256 devices in a mesh: row: 8 (over y, x_hi), col: 32 (over z, x_lo, core).
Axes of the slice: x: 4 (x_hi: 2, x_lo: 2; x = x_hi * 2 + x_lo), y: 4, z: 8, core: 2. Of those that a mesh axis runs over, the one named last changes fastest.
Arguments:
- tokens: bfloat16 [3072, 5120], P('col', 'row'), may hold values from -6 to 6
- up_blocks: bfloat16 [8, 32, 30, 4096], P('row', 'col'), may hold values from -0.21875 to 0.21875
- up_layout: int32 [8, 32, 30], P('row', 'col'), may hold values from 0 to 99, as said below
- up_counts: int32 [8, 32], P('row', 'col'), may hold values from 1 to 30, as said below
- down_blocks: bfloat16 [8, 32, 30, 4096], P('row', 'col'), may hold values from -0.109375 to 0.109375
- down_layout: int32 [8, 32, 30], P('row', 'col'), may hold values from 0 to 99, as said below
- down_counts: int32 [8, 32], P('row', 'col'), may hold values from 1 to 30, as said below
- grad_out: bfloat16 [3072, 5120], P('col', 'row'), may hold values from -6 to 6
Outputs:
- grad_tokens: bfloat16 [3072, 5120], P('col', 'row')
- up_grad: float32 [8, 32, 30, 4096], P('row', 'col')
- down_grad: float32 [8, 32, 30, 4096], P('row', 'col')
The draws below stay inside these ranges and needn't reach their ends.
Inputs may be any that keep to these rules, and one draw needn't show every extreme that they name: `up_layout`: the 30 entries of one tile are distinct tile-local block numbers; number id stands for block row id // 10 and block column id % 10 of the tile. `down_layout`: the 30 entries of one tile are distinct tile-local block numbers; number id stands for hidden block id % 10 and model-width block id // 10 of the tile. `up_counts`: some tile has all 30 slots live. `down_counts`: some tile has all 30 slots live.
All inputs are finite; a program needn't handle non-finite values.
Results may differ from the reference program's by a relative error of at most 0.0049.
Values may be sent and summed in bfloat16 or wider, within the bound.
A program may use at most 192 MiB of HBM per device.

```python
import jax
import jax.numpy as jnp
from jax import lax

D = 5120
FF = 20480
BLOCK = 64
TOKENS = 3072
DB_DEV = 10
FB_DEV = 10
CAP = 30
N_ROW = 8
N_COL = 32


def tile_layout(key):
    key_list = jax.random.split(key, N_ROW * N_COL)
    chosen_ids = jax.vmap(lambda each_key: jax.random.permutation(each_key, DB_DEV * FB_DEV)[:CAP])(key_list)
    return chosen_ids.reshape(N_ROW, N_COL, CAP).astype(jnp.int32)


def tile_counts(key):
    first_key, second_key = jax.random.split(key)
    counts = jax.random.randint(first_key, (N_ROW * N_COL,), 1, CAP + 1)
    filled = jax.random.randint(second_key, (), 0, N_ROW * N_COL)
    counts = jnp.where(jnp.arange(N_ROW * N_COL) == filled, CAP, counts)
    return counts.reshape(N_ROW, N_COL).astype(jnp.int32)


def draw_up_layout(key, part):
    key = jax.random.fold_in(key, 11)
    return tile_layout(key)


def draw_up_counts(key, part):
    key = jax.random.fold_in(key, 12)
    return tile_counts(key)


def draw_down_layout(key, part):
    key = jax.random.fold_in(key, 13)
    return tile_layout(key)


def draw_down_counts(key, part):
    key = jax.random.fold_in(key, 14)
    return tile_counts(key)


def block_scale(own_key, extent, pieces, least, high):
    def one(dim, parts):
        steps = jax.random.uniform(jax.random.fold_in(jax.random.fold_in(own_key, 6), dim), (parts,), jnp.float32, least / len(pieces), high / len(pieces))
        return jnp.repeat(jnp.exp(steps), extent[dim] // parts).reshape((-1,) + (1,) * (len(extent) - dim - 1))

    level = one(*pieces[0])
    for cut in pieces[1:]:
        level = level * one(*cut)
    return level


def scatter_about(own_key, extent, scale, bound, shards=(), held_as=jnp.bfloat16):
    loudness = block_scale(own_key, extent, shards, -0.22, 0.18) if shards else 1.0
    drawn = jax.random.normal(own_key, extent, jnp.float32) * scale * loudness
    return jnp.minimum(jnp.maximum(drawn, -bound), bound).astype(held_as)


def setup_inputs(seed: int = 0) -> dict:
    seeds = jax.random.split(jax.random.key(seed), 9)
    return {
        "tokens": scatter_about(seeds[0], (TOKENS, D), 1.0, 6.0, ((0, 32), (1, 8))),
        "up_blocks": scatter_about(seeds[1], (N_ROW, N_COL, CAP, BLOCK * BLOCK), (D * 3 // 20) ** -0.5, 0.21875, ((0, 8), (1, 32))),
        "up_layout": draw_up_layout(jax.random.fold_in(seeds[8], 71), 0),
        "up_counts": draw_up_counts(jax.random.fold_in(seeds[8], 71), 0),
        "down_blocks": scatter_about(seeds[4], (N_ROW, N_COL, CAP, BLOCK * BLOCK), (FF * 3 // 20) ** -0.5, 0.109375, ((0, 8), (1, 32))),
        "down_layout": draw_down_layout(jax.random.fold_in(seeds[8], 71), 0),
        "down_counts": draw_down_counts(jax.random.fold_in(seeds[8], 71), 0),
        "grad_out": scatter_about(seeds[7], (TOKENS, D), 1.0, 6.0, ((0, 32), (1, 8))),
    }


GELU_C = 0.7978845608028654
GELU_A = 0.044715

def gelu_value(values):
    return 0.5 * values * (1.0 + jnp.tanh(GELU_C * (values + GELU_A * values * values * values)))

def gelu_slope(values):
    tanh_part = jnp.tanh(GELU_C * (values + GELU_A * values * values * values))
    return 0.5 * (1.0 + tanh_part) + 0.5 * values * (1.0 - tanh_part * tanh_part) * GELU_C * (1.0 + 3.0 * GELU_A * values * values)

def tile_term(source, blocks, pick_ids, put_ids, live_mask, put_count, transpose):
    chosen = jnp.take(source, pick_ids, axis=1).astype(jnp.float32)
    einsum_form = 'tsn,skn->tsk' if transpose else 'tsk,skn->tsn'
    products = jnp.einsum(einsum_form, chosen, blocks.astype(jnp.float32), precision=lax.Precision.HIGHEST)
    targets = jnp.arange(put_count, dtype=jnp.int32)
    placement = ((put_ids[:, None] == targets[None, :]) & live_mask[:, None]).astype(jnp.float32)
    result = jnp.einsum('tsn,sf->tfn', products, placement, precision=lax.Precision.HIGHEST)
    return result.reshape(result.shape[0], put_count * result.shape[2])

def tile_grad(left_cols, right_cols, pick_left, pick_right, live_mask):
    left_sel = jnp.take(left_cols, pick_left, axis=1).astype(jnp.float32)
    right_sel = jnp.take(right_cols, pick_right, axis=1).astype(jnp.float32)
    grads = jnp.einsum('tsk,tsn->skn', left_sel, right_sel, precision=lax.Precision.HIGHEST)
    return grads * live_mask[:, None, None].astype(jnp.float32)

def reference(tokens, up_blocks, up_layout, up_counts, down_blocks, down_layout, down_counts, grad_out):
    row_count = tokens.shape[0]
    slot_ids = jnp.arange(CAP, dtype=jnp.int32)
    up_square = up_blocks.reshape(N_ROW, N_COL, CAP, BLOCK, BLOCK)
    down_square = down_blocks.reshape(N_ROW, N_COL, CAP, BLOCK, BLOCK)
    tok_groups = tokens.reshape(row_count, N_ROW, DB_DEV, BLOCK)
    out_groups = grad_out.reshape(row_count, N_ROW, DB_DEV, BLOCK)

    def row_sum(source_groups, blocks, layout, counts, transpose):

        def one_row(running, r_index):
            source = jnp.take(source_groups, r_index, axis=1)

            def one_tile(c_index):
                tile_ids = layout[r_index, c_index]
                live_mask = slot_ids < counts[r_index, c_index]
                return tile_term(source, blocks[r_index, c_index], tile_ids // FB_DEV, tile_ids % FB_DEV, live_mask, FB_DEV, transpose)
            terms = lax.map(one_tile, jnp.arange(N_COL, dtype=jnp.int32))
            partial_term = jnp.transpose(terms, (1, 0, 2)).reshape(row_count, FF)
            return (running + partial_term, None)
        running, _ = lax.scan(one_row, jnp.zeros((row_count, FF), jnp.float32), jnp.arange(N_ROW, dtype=jnp.int32))
        return running
    pre = row_sum(tok_groups, up_square, up_layout, up_counts, False)
    hidden = gelu_value(pre).astype(jnp.bfloat16)
    hidden_grad = row_sum(out_groups, down_square, down_layout, down_counts, True)
    pre_grad = (hidden_grad * gelu_slope(pre)).astype(jnp.bfloat16)
    grad_groups = pre_grad.reshape(row_count, N_COL, FB_DEV, BLOCK)
    hidden_groups = hidden.reshape(row_count, N_COL, FB_DEV, BLOCK)

    def one_col(running, c_index):
        source = jnp.take(grad_groups, c_index, axis=1)

        def one_tile(r_index):
            tile_ids = up_layout[r_index, c_index]
            live_mask = slot_ids < up_counts[r_index, c_index]
            return tile_term(source, up_square[r_index, c_index], tile_ids % FB_DEV, tile_ids // FB_DEV, live_mask, DB_DEV, True)
        terms = lax.map(one_tile, jnp.arange(N_ROW, dtype=jnp.int32))
        return (running + jnp.transpose(terms, (1, 0, 2)).reshape(row_count, D), None)
    input_total, _ = lax.scan(one_col, jnp.zeros((row_count, D), jnp.float32), jnp.arange(N_COL, dtype=jnp.int32))
    grad_tokens = input_total.astype(jnp.bfloat16)

    def pair_grads(pair_index):
        r_index = pair_index // N_COL
        c_index = pair_index % N_COL
        tok_cols = jnp.take(tok_groups, r_index, axis=1)
        out_cols = jnp.take(out_groups, r_index, axis=1)
        grad_cols = jnp.take(grad_groups, c_index, axis=1)
        hidden_cols = jnp.take(hidden_groups, c_index, axis=1)
        up_ids = up_layout[r_index, c_index]
        down_ids = down_layout[r_index, c_index]
        up_live = slot_ids < up_counts[r_index, c_index]
        down_live = slot_ids < down_counts[r_index, c_index]
        up_part = tile_grad(tok_cols, grad_cols, up_ids // FB_DEV, up_ids % FB_DEV, up_live)
        down_part = tile_grad(hidden_cols, out_cols, down_ids % FB_DEV, down_ids // FB_DEV, down_live)
        return (up_part, down_part)
    up_all, down_all = lax.map(pair_grads, jnp.arange(N_ROW * N_COL, dtype=jnp.int32))
    up_grad = up_all.reshape(N_ROW, N_COL, CAP, BLOCK * BLOCK)
    down_grad = down_all.reshape(N_ROW, N_COL, CAP, BLOCK * BLOCK)
    return (grad_tokens, up_grad, down_grad)
```

```python
import jax
import jax.numpy as jnp
from jax import lax
from jax.experimental import pallas as pl
from jax.experimental.pallas import tpu as pltpu
from jax.sharding import PartitionSpec as P

BLOCK = 64
CAP = 30
PAIRS = CAP // 2
NB = 10
ROWS = PAIRS * BLOCK
EXTRA = 16
TOK = 96
FEAT = NB * BLOCK
GROUP = 4 * TOK
SHIFT = 1024
SLAB = 5 * FEAT
MESH = pl.DeviceIdType.MESH
BF16 = jnp.bfloat16
F32 = jnp.float32

GELU_C = 0.7978845608028654
GELU_A = 0.044715


class Place:
    def __init__(self):
        self.p = lax.axis_index("row")
        col = lax.axis_index("col")
        self.z, self.xl, self.core = col // 4, (col // 2) % 2, col % 2
        self.y, self.xh = self.p // 2, self.p % 2
        self.f = (self.z + 7) % 8

    def col(self, z, xl, core):
        return z * 4 + xl * 2 + core

    def sibling(self):
        return (self.p, self.col(self.z, self.xl, 1 - self.core))

    def partner_lo(self):
        return (self.p, self.col(self.z, 1 - self.xl, self.core))

    def partner_hi(self):
        return (self.y * 2 + 1 - self.xh, self.col(self.z, self.xl, self.core))

    def along_y(self, step):
        return (((self.y + step + 4) % 4) * 2 + self.xh, self.col(self.z, self.xl, self.core))

    def along_z(self, step):
        return (self.p, self.col((self.z + step + 8) % 8, self.xl, self.core))

    def out_to(self):
        return ((self.z + 4 * self.core) % 8, self.col((self.p + 1) % 8, self.xl, self.core))

    def back_to(self):
        return (self.f, self.col((self.p + 8 - 4 * self.core) % 8, self.xl, self.core))

    def feature(self, step):
        return (self.z + step + 7 + 8) % 8


class Copies:
    def __init__(self, send_sems, recv_sems):
        self.send_sems, self.recv_sems = send_sems, recv_sems
        self.number = 0
        self.started = []

    def start(self, src, dst, device):
        copy = pltpu.make_async_remote_copy(
            src_ref=src,
            dst_ref=dst,
            send_sem=self.send_sems.at[self.number],
            recv_sem=self.recv_sems.at[self.number],
            device_id=device,
            device_id_type=MESH,
        )
        self.number += 1
        copy.start()
        self.started.append(copy)
        return copy

    def finish(self):
        for copy in self.started:
            copy.wait_send()


def greet(place):
    devices = [
        place.sibling(),
        place.partner_lo(),
        place.partner_hi(),
        place.along_y(1),
        place.along_y(-1),
        place.along_z(1),
        place.along_z(-1),
        place.out_to(),
        place.back_to(),
    ]
    barrier = pltpu.get_barrier_semaphore()
    for device in devices:
        pl.semaphore_signal(barrier, inc=1, device_id=device, device_id_type=MESH)
    pl.semaphore_wait(barrier, len(devices))


def gather_kernel(tok, out, pay, held, strip, own_sem, send_sems, recv_sems):
    place = Place()
    z, y, xh, xl, core = place.z, place.y, place.xh, place.xl, place.core
    greet(place)
    copies = Copies(send_sems, recv_sems)
    go = copies.start

    perm_tok = go(tok, held.at[0, place.p, core, xl], place.out_to())
    perm_out = go(out, held.at[1, place.p, core, xl], place.out_to())
    swap = go(pay, strip.at[:, y, xh], place.partner_hi())
    own = pltpu.make_async_copy(pay, strip.at[:, y, xh], own_sem)
    own.start()

    def toks(step):
        return held.at[0, place.feature(step), core]

    def outs(step):
        return held.at[1, place.feature(step), core, xl]

    def both_outs(step):
        return held.at[1, place.feature(step), core]

    def to_core(ref):
        return go(ref, ref, place.sibling())

    lo_outs, core_toks, core_outs = {}, [], []

    perm_tok.wait_recv()
    mine = held.at[0, place.f, core, xl]
    lo_tok = go(mine, mine, place.partner_lo())
    perm_out.wait_recv()
    right_out = go(outs(0), outs(0), place.along_z(1))
    left_out = go(outs(0), outs(0), place.along_z(-1))
    lo_outs[0] = go(outs(0), outs(0), place.partner_lo())
    lo_tok.wait_recv()
    right_tok = go(toks(0), toks(0), place.along_z(1))
    left_tok = go(toks(0), toks(0), place.along_z(-1))
    core_toks.append(to_core(toks(0)))

    swap.wait_recv()
    own.wait()
    ys = []
    for w in range(2):
        bundle = strip.at[w, y]
        ys.append((go(bundle, bundle, place.along_y(1)), go(bundle, bundle, place.along_y(-1))))

    for step in (1, 2, 3, 4):
        if step < 4:
            right_out.wait_recv()
            ref = outs(-step)
            if step < 3:
                right_out = go(ref, ref, place.along_z(1))
            lo_outs[-step] = go(ref, ref, place.partner_lo())
        left_out.wait_recv()
        ref = outs(step)
        if step < 4:
            left_out = go(ref, ref, place.along_z(-1))
        lo_outs[step] = go(ref, ref, place.partner_lo())

        right_tok.wait_recv()
        ref = toks(-step)
        if step < 4:
            right_tok = go(ref, ref, place.along_z(1))
        core_toks.append(to_core(ref))
        if step < 4:
            left_tok.wait_recv()
            ref = toks(step)
            if step < 3:
                left_tok = go(ref, ref, place.along_z(-1))
            core_toks.append(to_core(ref))

        if step == 1:
            up_far = strip.at[0, (y + 3) % 4]
            down_far = strip.at[1, (y + 1) % 4]
            ys[0][0].wait_recv()
            far_up = go(up_far, up_far, place.along_y(1))
            ys[1][1].wait_recv()
            far_down = go(down_far, down_far, place.along_y(-1))
        for done in ((0,), (-1, 1), (-2, 2), (-3, 3))[step - 1]:
            lo_outs[done].wait_recv()
            core_outs.append(to_core(both_outs(done)))
    lo_outs[4].wait_recv()
    core_outs.append(to_core(both_outs(4)))
    ys[0][1].wait_recv()
    ys[1][0].wait_recv()
    far_up.wait_recv()
    far_down.wait_recv()
    for copy in core_toks + core_outs:
        copy.wait_recv()
    copies.finish()


GATHER_COPIES = 3 + 1 + 2 * 7 + 8 + 16 + 6


def compute_kernel(place_ref, take_ref, held, strip, tok_part, up_part, down_part, up_dense, down_dense, blocks, pre, slope_part, hidden, pre_grad, grads):
    zeros = jnp.zeros((BLOCK, 128), BF16)
    blocks[ROWS : ROWS + BLOCK, :] = zeros
    blocks[SHIFT + ROWS : SHIFT + ROWS + BLOCK, :] = zeros

    def load_blocks(which, tile):
        data = strip[which, tile, 0:ROWS, :]
        blocks[0:ROWS, :] = data
        blocks[SHIFT : SHIFT + ROWS, :] = jnp.concatenate([data[:, BLOCK:], data[:, :BLOCK]], axis=1)

    def one_tile(tile, carry):
        load_blocks(0, tile)
        for i in range(NB):
            for j in range(NB):
                start = pl.multiple_of(place_ref[tile, i * NB + j], BLOCK)
                half = (j % 2) * BLOCK
                up_dense[tile, i * BLOCK : (i + 1) * BLOCK, j * BLOCK : (j + 1) * BLOCK] = blocks[
                    pl.ds(start, BLOCK), half : half + BLOCK
                ]
        load_blocks(1, tile)
        for i in range(NB):
            for j in range(NB):
                start = pl.multiple_of(place_ref[8 + tile, i * NB + j], BLOCK)
                half = (i % 2) * BLOCK
                down_dense[j * BLOCK : (j + 1) * BLOCK, i * BLOCK : (i + 1) * BLOCK] = blocks[
                    pl.ds(start, BLOCK), half : half + BLOCK
                ]
        pre[...] += jnp.dot(held[0, tile], up_dense[tile], preferred_element_type=F32)
        slope_part[...] += lax.dot_general(
            held[1, tile], down_dense[...], (((1,), (1,)), ((), ())), preferred_element_type=F32
        )
        return carry

    pre[...] = jnp.zeros_like(pre)
    slope_part[...] = jnp.zeros_like(slope_part)
    lax.fori_loop(0, 8, one_tile, 0)

    def activate(index, carry):
        rows = pl.ds(pl.multiple_of(index * 32, 32), 32)
        v = pre[rows, :]
        t = jnp.tanh(GELU_C * (v + GELU_A * v * v * v))
        hidden[rows, :] = (0.5 * v * (1.0 + t)).astype(BF16)
        slope = 0.5 * (1.0 + t) + 0.5 * v * (1.0 - t * t) * GELU_C * (1.0 + 3.0 * GELU_A * v * v)
        pre_grad[rows, :] = (slope_part[rows, :] * slope).astype(BF16)
        return carry

    lax.fori_loop(0, GROUP // 32, activate, 0)

    def extract(product, row, target, tile):
        product = product.astype(BF16)
        for slab in range(5):
            data = product[:, slab * 128 : (slab + 1) * 128]
            grads[slab * FEAT : (slab + 1) * FEAT, :] = data
            grads[SLAB + slab * FEAT : SLAB + (slab + 1) * FEAT, :] = jnp.concatenate(
                [data[:, BLOCK:], data[:, :BLOCK]], axis=1
            )
        for slot in range(CAP):
            start = pl.multiple_of(take_ref[row, slot], BLOCK)
            half = (slot % 2) * BLOCK
            place = (slot // 2) * BLOCK
            target[tile, place : place + BLOCK, half : half + BLOCK] = grads[pl.ds(start, BLOCK), half : half + BLOCK]

    def grad_tile(tile, carry):
        tok_part[tile] = lax.dot_general(
            pre_grad[...], up_dense[tile], (((1,), (1,)), ((), ())), preferred_element_type=F32
        ).astype(BF16)
        extract(
            lax.dot_general(held[0, tile], pre_grad[...], (((0,), (0,)), ((), ())), preferred_element_type=F32),
            tile, up_part, tile,
        )
        extract(
            lax.dot_general(hidden[...], held[1, tile], (((0,), (0,)), ((), ())), preferred_element_type=F32),
            8 + tile, down_part, tile,
        )
        return carry

    lax.fori_loop(0, 8, grad_tile, 0)


def add(*parts):
    total = parts[0].astype(F32)
    for part in parts[1:]:
        total = total + part.astype(F32)
    return total


def scatter_kernel(
    tok_part, up_part, down_part, tok_out, up_out, down_out,
    from_core, summed, right_in, left_in, right_far, left_far, lo_out, lo_in, home,
    y_far, y_right, y_left, y_send, hi_out, hi_in, send_sems, recv_sems,
):
    place = Place()
    y, xh, xl, core = place.y, place.xh, place.xl, place.core
    greet(place)
    copies = Copies(send_sems, recv_sems)
    go = copies.start

    core_in = {}
    for step in (4, 3, -3, 2, -2, 1, -1, 0):
        f = place.feature(step)
        core_in[step] = go(tok_part.at[f, 1 - core], from_core.at[f], place.sibling())

    far_up = go(up_part.at[(y + 2) % 4], y_far.at[0], place.along_y(1))
    far_down = go(down_part.at[(y + 2) % 4], y_far.at[1], place.along_y(-1))
    up_left = go(up_part.at[(y + 3) % 4], y_left.at[0], place.along_y(-1))
    down_right = go(down_part.at[(y + 1) % 4], y_right.at[1], place.along_y(1))

    def sum_core(step):
        f = place.feature(step)
        core_in[step].wait_recv()
        for half in range(2):
            summed[f, half] = add(tok_part[f, core, half], from_core[f, half]).astype(BF16)
        return f

    f = sum_core(4)
    go_right = go(summed.at[f, 0], right_far, place.along_z(1))
    go_left = go(summed.at[f, 1], left_far, place.along_z(-1))
    for step in (3, 2, 1):
        f = sum_core(step)
        go_right.wait_recv()
        if step == 3:
            summed[f, 0] = add(summed[f, 0], right_far[...]).astype(BF16)
        else:
            for half in range(2):
                summed[f, half] = add(summed[f, half], right_in[3 - step - 1, half]).astype(BF16)
        go_right = go(summed.at[f], right_in.at[3 - step], place.along_z(1))
        f = sum_core(-step)
        go_left.wait_recv()
        if step == 3:
            summed[f, 1] = add(summed[f, 1], left_far[...]).astype(BF16)
        else:
            for half in range(2):
                summed[f, half] = add(summed[f, half], left_in[3 - step - 1, half]).astype(BF16)
        go_left = go(summed.at[f], left_in.at[3 - step], place.along_z(-1))
        if step == 3:
            far_up.wait_recv()
            for side in range(2):
                y_send[0, side] = add(up_part[(y + 1) % 4, side], y_far[0, side]).astype(BF16)
            up_right = go(y_send.at[0], y_right.at[0], place.along_y(1))
            far_down.wait_recv()
            for side in range(2):
                y_send[1, side] = add(down_part[(y + 3) % 4, side], y_far[1, side]).astype(BF16)
            down_left = go(y_send.at[1], y_left.at[1], place.along_y(-1))

    f = sum_core(0)
    go_right.wait_recv()
    go_left.wait_recv()
    other = 1 - xl
    lo_out[...] = add(
        tok_part[f, core, other], from_core[f, other], right_in[2, other], left_in[2, other]
    ).astype(BF16)
    lo = go(lo_out, lo_in, place.partner_lo())

    up_left.wait_recv()
    up_right.wait_recv()
    down_left.wait_recv()
    down_right.wait_recv()
    far = 1 - xh
    hi_out[0] = add(up_part[y, far], y_left[0, far], y_right[0, far]).astype(BF16)
    hi_out[1] = add(down_part[y, far], y_left[1, far], y_right[1, far]).astype(BF16)
    hi = go(hi_out, hi_in, place.partner_hi())

    lo.wait_recv()
    home[...] = add(
        tok_part[f, core, xl], from_core[f, xl], right_in[2, xl], left_in[2, xl], lo_in[...]
    ).astype(BF16)
    back = go(home, tok_out, place.back_to())

    hi.wait_recv()
    up_out[...] = add(up_part[y, xh], y_left[0, xh], y_right[0, xh], hi_in[0])
    down_out[...] = add(down_part[y, xh], y_left[1, xh], y_right[1, xh], hi_in[1])
    back.wait_recv()
    copies.finish()


SCATTER_COPIES = 8 + 4 + 8 + 2 + 3


def vmem(count):
    return [pl.BlockSpec(memory_space=pltpu.VMEM)] * count


def hbm(count):
    return [pl.BlockSpec(memory_space=pl.ANY)] * count


def sds(shape, dtype=BF16):
    return jax.ShapeDtypeStruct(shape, dtype)


def payload(blocks, layout, counts):
    pairs = blocks[0, 0].reshape(PAIRS, 2, BLOCK, BLOCK).transpose(0, 2, 1, 3).reshape(ROWS, 2 * BLOCK)
    ids = layout[0, 0]
    slots = jnp.arange(CAP, dtype=jnp.int32)
    hit = (ids[:, None] == jnp.arange(128, dtype=jnp.int32)[None, :]) & (slots < counts[0, 0])[:, None]
    slot_of = CAP + jnp.sum(jnp.where(hit, slots[:, None] - CAP, 0), axis=0)
    extra = jnp.zeros((EXTRA, 128), jnp.int32).at[0].set(slot_of).at[1, :CAP].set(ids)
    return jnp.concatenate([pairs, extra.astype(BF16)], axis=0)


def offsets(extra):
    numbers = jnp.arange(128, dtype=jnp.int32)
    slot_of, ids = extra[:, :, 0].astype(jnp.int32), extra[:, :, 1].astype(jnp.int32)
    odd = jnp.stack([numbers % NB % 2, numbers // NB % 2])[:, None, :]
    place = ((slot_of % 2 + odd) % 2) * SHIFT + (slot_of // 2) * BLOCK
    i, j = ids // NB, ids % NB
    lane = jnp.stack([j[0], i[1]])
    row = jnp.stack([i[0], j[1]])
    take = ((lane % 2 + numbers % 2) % 2) * SLAB + (lane // 2) * FEAT + row * BLOCK
    return place.reshape(16, 128), take.reshape(16, 128)


def body(tokens, up_blocks, up_layout, up_counts, down_blocks, down_layout, down_counts, grad_out):
    pay = jnp.stack([payload(up_blocks, up_layout, up_counts), payload(down_blocks, down_layout, down_counts)])
    held, strip = pl.pallas_call(
        gather_kernel,
        out_shape=(sds((2, 8, 2, 2, TOK, FEAT)), sds((2, 4, 2, ROWS + EXTRA, 128))),
        in_specs=hbm(3),
        out_specs=tuple(hbm(2)),
        scratch_shapes=[
            pltpu.SemaphoreType.DMA,
            pltpu.SemaphoreType.DMA((GATHER_COPIES,)),
            pltpu.SemaphoreType.DMA((GATHER_COPIES,)),
        ],
        compiler_params=pltpu.CompilerParams(collective_id=0, has_side_effects=True),
        name="gather",
    )(tokens, grad_out, pay)
    held = held.reshape(2, 8, GROUP, FEAT)
    strip = strip.reshape(2, 8, ROWS + EXTRA, 128)
    place, take = offsets(strip[:, :, ROWS : ROWS + 2])
    tok_part, up_part, down_part = pl.pallas_call(
        compute_kernel,
        out_shape=(sds((8, GROUP, FEAT)), sds((8, ROWS, 128)), sds((8, ROWS, 128))),
        in_specs=[pl.BlockSpec(memory_space=pltpu.SMEM)] * 2 + vmem(2),
        out_specs=tuple(vmem(3)),
        scratch_shapes=[
            pltpu.VMEM((8, FEAT, FEAT), BF16),
            pltpu.VMEM((FEAT, FEAT), BF16),
            pltpu.VMEM((2 * SHIFT, 128), BF16),
            pltpu.VMEM((GROUP, FEAT), F32),
            pltpu.VMEM((GROUP, FEAT), F32),
            pltpu.VMEM((GROUP, FEAT), BF16),
            pltpu.VMEM((GROUP, FEAT), BF16),
            pltpu.VMEM((2 * SLAB, 128), BF16),
        ],
        compiler_params=pltpu.CompilerParams(vmem_limit_bytes=56 * 2**20),
        name="compute",
    )(place, take, held, strip)
    tok_grad, up_sum, down_sum = pl.pallas_call(
        scatter_kernel,
        out_shape=(sds((TOK, FEAT)), sds((ROWS, 128), F32), sds((ROWS, 128), F32)),
        in_specs=vmem(3),
        out_specs=tuple(vmem(3)),
        scratch_shapes=[
            pltpu.VMEM((8, 2, TOK, FEAT), BF16),
            pltpu.VMEM((8, 2, TOK, FEAT), BF16),
            pltpu.VMEM((3, 2, TOK, FEAT), BF16),
            pltpu.VMEM((3, 2, TOK, FEAT), BF16),
            pltpu.VMEM((TOK, FEAT), BF16),
            pltpu.VMEM((TOK, FEAT), BF16),
            pltpu.VMEM((TOK, FEAT), BF16),
            pltpu.VMEM((TOK, FEAT), BF16),
            pltpu.VMEM((TOK, FEAT), BF16),
            pltpu.VMEM((2, 2, ROWS, 128), BF16),
            pltpu.VMEM((2, 2, ROWS, 128), BF16),
            pltpu.VMEM((2, 2, ROWS, 128), BF16),
            pltpu.VMEM((2, 2, ROWS, 128), BF16),
            pltpu.VMEM((2, ROWS, 128), BF16),
            pltpu.VMEM((2, ROWS, 128), BF16),
            pltpu.SemaphoreType.DMA((SCATTER_COPIES,)),
            pltpu.SemaphoreType.DMA((SCATTER_COPIES,)),
        ],
        compiler_params=pltpu.CompilerParams(collective_id=1, has_side_effects=True, vmem_limit_bytes=48 * 2**20),
        name="scatter",
    )(
        tok_part.reshape(8, 2, 2, TOK, FEAT),
        up_part.reshape(4, 2, ROWS, 128),
        down_part.reshape(4, 2, ROWS, 128),
    )

    def slots(total, counts):
        flat = total.reshape(PAIRS, BLOCK, 2, BLOCK).transpose(0, 2, 1, 3).reshape(CAP, BLOCK * BLOCK)
        live = jnp.arange(CAP, dtype=jnp.int32) < counts[0, 0]
        return jnp.where(live[:, None], flat, 0.0)[None, None]

    return tok_grad, slots(up_sum, up_counts), slots(down_sum, down_counts)


def solution(mesh):
    in_specs = (
        P("col", "row"),
        P("row", "col", None, None),
        P("row", "col", None),
        P("row", "col"),
        P("row", "col", None, None),
        P("row", "col", None),
        P("row", "col"),
        P("col", "row"),
    )
    out_specs = (P("col", "row"), P("row", "col", None, None), P("row", "col", None, None))
    return jax.shard_map(body, mesh=mesh, in_specs=in_specs, out_specs=out_specs, check_vma=False)
```

```python
import jax
import jax.numpy as jnp
from jax import lax
from jax.experimental import pallas as pl
from jax.experimental.pallas import tpu as pltpu
from jax.sharding import PartitionSpec as P

BLOCK = 64
CAP = 30
PAIRS = CAP // 2
NB = 10
ROWS = PAIRS * BLOCK
EXTRA = 16
TOK = 96
FEAT = NB * BLOCK
GROUP = 4 * TOK
SHIFT = 16
SLAB = 5 * NB
MESH = pl.DeviceIdType.MESH
BF16 = jnp.bfloat16
F32 = jnp.float32

GELU_C = 0.7978845608028654
GELU_A = 0.044715


class Place:
    def __init__(self):
        self.p = lax.axis_index("row")
        col = lax.axis_index("col")
        self.z, self.xl, self.core = col // 4, (col // 2) % 2, col % 2
        self.y, self.xh = self.p // 2, self.p % 2
        self.f = (self.z + 7) % 8

    def col(self, z, xl, core):
        return z * 4 + xl * 2 + core

    def sibling(self):
        return (self.p, self.col(self.z, self.xl, 1 - self.core))

    def partner_lo(self):
        return (self.p, self.col(self.z, 1 - self.xl, self.core))

    def partner_hi(self):
        return (self.y * 2 + 1 - self.xh, self.col(self.z, self.xl, self.core))

    def along_y(self, step):
        return (((self.y + step + 4) % 4) * 2 + self.xh, self.col(self.z, self.xl, self.core))

    def along_z(self, step):
        return (self.p, self.col((self.z + step + 8) % 8, self.xl, self.core))

    def out_to(self):
        return ((self.z + 4 * self.core) % 8, self.col((self.p + 1) % 8, self.xl, self.core))

    def back_to(self):
        return (self.f, self.col((self.p + 8 - 4 * self.core) % 8, self.xl, self.core))

    def feature(self, step):
        return (self.z + step + 7 + 8) % 8


class Copies:
    def __init__(self, send_sems, recv_sems):
        self.send_sems, self.recv_sems = send_sems, recv_sems
        self.number = 0
        self.made = []

    def reserve(self, count):
        first = self.number
        self.number += count
        return first

    def copy(self, src, dst, device, index):
        return pltpu.make_async_remote_copy(
            src_ref=src,
            dst_ref=dst,
            send_sem=self.send_sems.at[index],
            recv_sem=self.recv_sems.at[index],
            device_id=device,
            device_id_type=MESH,
        )

    def start(self, src, dst, device):
        copy = self.copy(src, dst, device, self.reserve(1))
        copy.start()
        self.made.append(copy)
        return copy

    def started(self, src, dst, device, index):
        copy = self.copy(src, dst, device, index)
        self.made.append(copy)
        return copy

    def finish(self):
        for copy in self.made:
            copy.wait_send()


def greet(place):
    devices = [
        place.sibling(),
        place.partner_lo(),
        place.partner_hi(),
        place.along_y(1),
        place.along_y(-1),
        place.along_z(1),
        place.along_z(-1),
        place.out_to(),
        place.back_to(),
    ]
    barrier = pltpu.get_barrier_semaphore()
    for device in devices:
        pl.semaphore_signal(barrier, inc=1, device_id=device, device_id_type=MESH)
    pl.semaphore_wait(barrier, len(devices))


def add(*parts):
    total = parts[0].astype(F32)
    for part in parts[1:]:
        total = total + part.astype(F32)
    return total


def kernel(
    tok, out, pay, meta,
    tok_out, up_out, down_out,
    held, strip, numbers, numbers_sm, dense, blocks, pre, slope_part, hidden, pre_grad, grads,
    own_tok, core_send, from_core, tok_send, right_in, left_in, right_far, left_far, lo_out, lo_in, home,
    part, y_far, y_right, y_left, y_send, hi_out, hi_in,
    meta_sems, send_sems, recv_sems,
):
    place = Place()
    z, y, xh, xl, core = place.z, place.y, place.xh, place.xl, place.core
    mine, twin = place.p, y * 2 + 1 - xh
    right, left = place.along_y(1), place.along_y(-1)
    greet(place)
    copies = Copies(send_sems, recv_sems)
    go = copies.start

    perm_tok = go(tok, held.at[0, place.p, core, xl], place.out_to())
    perm_out = go(out, held.at[1, place.p, core, xl], place.out_to())
    swap_meta = go(meta, numbers.at[mine], place.partner_hi())
    swap = go(pay, strip.at[:, mine], place.partner_hi())

    def to_scalars(source, tile, index):
        copy = pltpu.make_async_copy(source, numbers_sm.at[tile], meta_sems.at[index])
        copy.start()
        return copy

    def fill(which, tile, data):
        turned = jnp.concatenate([data[:, BLOCK:], data[:, :BLOCK]], axis=1)
        blocks[0:PAIRS] = data.reshape(PAIRS, BLOCK, 128)
        blocks[SHIFT : SHIFT + PAIRS] = turned.reshape(PAIRS, BLOCK, 128)
        for i in range(NB):
            for j in range(NB):
                half = (j % 2) * BLOCK
                dense[which, tile, i * BLOCK : (i + 1) * BLOCK, j * BLOCK : (j + 1) * BLOCK] = blocks[
                    numbers_sm[tile, which, i * NB + j], :, half : half + BLOCK
                ]

    def fill_tiles(tiles):
        def step(index, carry):
            which, tile = index % 2, tiles(index // 2)
            fill(which, tile, strip[which, tile])
            return carry

        return step

    zeros = jnp.zeros((BLOCK, 128), BF16)
    blocks[PAIRS] = zeros
    blocks[SHIFT + PAIRS] = zeros
    pre[...] = jnp.zeros_like(pre)
    slope_part[...] = jnp.zeros_like(slope_part)
    to_scalars(meta, mine, 0).wait()

    def fill_mine(which, carry):
        fill(which, mine, pay[which])
        return carry

    lax.fori_loop(0, 2, fill_mine, 0)

    def toks(step):
        return held.at[0, place.feature(step), core]

    def outs(step):
        return held.at[1, place.feature(step), core, xl]

    def both_outs(step):
        return held.at[1, place.feature(step), core]

    def to_core(ref):
        return go(ref, ref, place.sibling())

    lo_outs, core_toks, core_outs = {}, {}, {}

    perm_tok.wait_recv()
    piece = held.at[0, place.f, core, xl]
    lo_tok = go(piece, piece, place.partner_lo())
    meta_right = go(meta, numbers.at[mine], right)
    meta_left = go(meta, numbers.at[mine], left)
    near = [
        [go(pay.at[w], strip.at[w, mine], right), go(pay.at[w], strip.at[w, mine], left)] for w in range(2)
    ]

    lo_tok.wait_recv()
    right_tok = go(toks(0), toks(0), place.along_z(1))
    left_tok = go(toks(0), toks(0), place.along_z(-1))
    core_toks[0] = to_core(toks(0))

    swap_meta.wait_recv()
    ref = numbers.at[twin]
    twin_meta_right = go(ref, ref, right)
    twin_meta_left = go(ref, ref, left)
    twin_scalars = to_scalars(ref, twin, 1)
    swap.wait_recv()
    near_twin = []
    for w in range(2):
        ref = strip.at[w, twin]
        near_twin.append([go(ref, ref, right), go(ref, ref, left)])
    twin_scalars.wait()
    lax.fori_loop(0, 2, fill_tiles(lambda index: twin), 0)

    perm_out.wait_recv()
    right_out = go(outs(0), outs(0), place.along_z(1))
    left_out = go(outs(0), outs(0), place.along_z(-1))
    lo_outs[0] = go(outs(0), outs(0), place.partner_lo())

    def tile_at(step, side):
        return ((y + step + 4) % 4) * 2 + (xh + side) % 2

    def multiply(step):
        f = place.feature(step)
        t = held[0, f].reshape(GROUP, FEAT)
        pre[...] += jnp.dot(t, dense[0, f], preferred_element_type=F32)
        g = held[1, f].reshape(GROUP, FEAT)
        slope_part[...] += lax.dot_general(g, dense[1, f], (((1,), (1,)), ((), ())), preferred_element_type=F32)

    def multiply_ready(steps):
        for step in steps:
            core_toks[step].wait_recv()
            core_outs[step].wait_recv()

    far_copies = []
    for step in (1, 2, 3, 4):
        if step < 4:
            right_out.wait_recv()
            ref = outs(-step)
            if step < 3:
                right_out = go(ref, ref, place.along_z(1))
            lo_outs[-step] = go(ref, ref, place.partner_lo())
        left_out.wait_recv()
        ref = outs(step)
        if step < 4:
            left_out = go(ref, ref, place.along_z(-1))
        lo_outs[step] = go(ref, ref, place.partner_lo())

        right_tok.wait_recv()
        ref = toks(-step)
        if step < 4:
            right_tok = go(ref, ref, place.along_z(1))
        core_toks[-step] = to_core(ref)
        if step < 4:
            left_tok.wait_recv()
            ref = toks(step)
            if step < 3:
                left_tok = go(ref, ref, place.along_z(-1))
            core_toks[step] = to_core(ref)
        if step == 4:
            core_toks[4] = core_toks[-4]

        if step in (1, 2):
            side = step - 1
            came, met = (near, (meta_right, meta_left)) if side == 0 else (near_twin, (twin_meta_right, twin_meta_left))
            from_left, from_right = tile_at(-1, side), tile_at(1, side)
            met[0].wait_recv()
            far_meta = go(numbers.at[from_left], numbers.at[from_left], right)
            scalars = [to_scalars(numbers.at[from_left], from_left, 2 + 3 * side)]
            met[1].wait_recv()
            scalars.append(to_scalars(numbers.at[from_right], from_right, 3 + 3 * side))
            came[0][0].wait_recv()
            ref = strip.at[0, from_left]
            far_up = go(ref, ref, right)
            came[1][1].wait_recv()
            ref = strip.at[1, from_right]
            far_down = go(ref, ref, left)
            came[0][1].wait_recv()
            came[1][0].wait_recv()
            for copy in scalars:
                copy.wait()
            far_copies.append((far_meta, far_up, far_down))
            lax.fori_loop(0, 4, fill_tiles(lambda index, side=side: tile_at(2 * index - 1, side)), 0)
        for done in ((0,), (-1, 1), (-2, 2), (-3, 3))[step - 1]:
            lo_outs[done].wait_recv()
            core_outs[done] = to_core(both_outs(done))
        if step == 3:
            scalars = []
            for side in range(2):
                tile = tile_at(2, side)
                far_copies[side][0].wait_recv()
                scalars.append(to_scalars(numbers.at[tile], tile, 4 + 3 * side))
            for side in range(2):
                far_copies[side][1].wait_recv()
                far_copies[side][2].wait_recv()
            for copy in scalars:
                copy.wait()
            lax.fori_loop(0, 4, fill_tiles(lambda index: tile_at(2, index)), 0)
            multiply_ready((0, -1, 1))

            def near_features(index, carry):
                multiply(index - 1)
                return carry

            lax.fori_loop(0, 3, near_features, 0)
    lo_outs[4].wait_recv()
    core_outs[4] = to_core(both_outs(4))
    multiply_ready((-2, 2, -3, 3))

    def late_features(index, carry):
        multiply(2 + index + index // 2)
        return carry

    lax.fori_loop(0, 4, late_features, 0)
    multiply_ready((4,))
    multiply(4)

    def activate(index, carry):
        rows = pl.ds(pl.multiple_of(index * 32, 32), 32)
        v = pre[rows, :]
        t = jnp.tanh(GELU_C * (v + GELU_A * v * v * v))
        hidden[rows, :] = (0.5 * v * (1.0 + t)).astype(BF16)
        slope = 0.5 * (1.0 + t) + 0.5 * v * (1.0 - t * t) * GELU_C * (1.0 + 3.0 * GELU_A * v * v)
        pre_grad[rows, :] = (slope_part[rows, :] * slope).astype(BF16)
        return carry

    lax.fori_loop(0, GROUP // 32, activate, 0)

    def extract(product, which, tile):
        product = product.astype(BF16)
        for slab in range(5):
            data = product[:, slab * 128 : (slab + 1) * 128]
            turned = jnp.concatenate([data[:, BLOCK:], data[:, :BLOCK]], axis=1)
            grads[slab * NB : (slab + 1) * NB] = data.reshape(NB, BLOCK, 128)
            grads[SLAB + slab * NB : SLAB + (slab + 1) * NB] = turned.reshape(NB, BLOCK, 128)
        for slot in range(CAP):
            half = (slot % 2) * BLOCK
            at = (slot // 2) * BLOCK
            part[which, tile, at : at + BLOCK, half : half + BLOCK] = grads[
                numbers_sm[tile, 2 + which, slot], :, half : half + BLOCK
            ]

    def up_tile(tile):
        left_side = held[0, tile].reshape(GROUP, FEAT)
        extract(
            lax.dot_general(left_side, pre_grad[...], (((0,), (0,)), ((), ())), preferred_element_type=F32), 0, tile
        )

    def down_tile(tile):
        right_side = held[1, tile].reshape(GROUP, FEAT)
        extract(
            lax.dot_general(hidden[...], right_side, (((0,), (0,)), ((), ())), preferred_element_type=F32), 1, tile
        )

    half_rows = GROUP // 2

    def tok_feature(f, index):
        def rows_of(which_core):
            rows = pre_grad[pl.ds(pl.multiple_of(which_core * half_rows, half_rows), half_rows), :]
            return lax.dot_general(rows, dense[0, f], (((1,), (1,)), ((), ())), preferred_element_type=F32)

        core_send[f] = rows_of(1 - core).astype(BF16).reshape(2, TOK, FEAT)
        copies.copy(core_send.at[f], from_core.at[f], place.sibling(), index).start()
        own_tok[f] = rows_of(core).reshape(2, TOK, FEAT)

    core_first = copies.reserve(8)
    core_in = {}

    def tok_features(first, steps, step_of):
        def one(index, carry):
            tok_feature(place.feature(step_of(index)), core_first + first + index)
            return carry

        lax.fori_loop(0, len(steps), one, 0)
        for number, step in enumerate(steps):
            f = place.feature(step)
            core_in[step] = copies.started(
                core_send.at[f], from_core.at[f], place.sibling(), core_first + first + number
            )

    def far_tiles(index, carry):
        tile = tile_at(2, 1 - index)
        up_tile(tile)
        copies.copy(part.at[0, tile], y_far.at[0, 1 - index], right, far_first + index).start()
        down_tile(tile)
        copies.copy(part.at[1, tile], y_far.at[1, 1 - index], left, far_first + 2 + index).start()
        return carry

    far_first = copies.reserve(4)
    lax.fori_loop(0, 2, far_tiles, 0)
    far_in = [
        [copies.started(part.at[0, tile_at(2, side)], y_far.at[0, side], right, far_first + 1 - side) for side in range(2)],
        [copies.started(part.at[1, tile_at(2, side)], y_far.at[1, side], left, far_first + 3 - side) for side in range(2)],
    ]

    tok_features(0, (4, 3, -3), lambda index: 4 - index + (index // 2) * 3)

    def near_tiles(index, carry):
        tile = tile_at(1, 1 - index)
        down_tile(tile)
        copies.copy(part.at[1, tile], y_right.at[1, 1 - index], right, near_first + index).start()
        tile = tile_at(-1, 1 - index)
        up_tile(tile)
        copies.copy(part.at[0, tile], y_left.at[0, 1 - index], left, near_first + 2 + index).start()
        return carry

    near_first = copies.reserve(4)
    lax.fori_loop(0, 2, near_tiles, 0)
    down_right = [
        copies.started(part.at[1, tile_at(1, side)], y_right.at[1, side], right, near_first + 1 - side) for side in range(2)
    ]
    up_left = [
        copies.started(part.at[0, tile_at(-1, side)], y_left.at[0, side], left, near_first + 3 - side) for side in range(2)
    ]

    f = place.feature(4)
    core_in[4].wait_recv()
    tok_send[0] = add(own_tok[f], from_core[f]).astype(BF16)
    go_right = go(tok_send.at[0, 0], right_far, place.along_z(1))
    go_left = go(tok_send.at[0, 1], left_far, place.along_z(-1))

    tok_features(3, (2, -2), lambda index: 2 + 4 * index)

    def pass_on(step):
        nonlocal go_right, go_left
        f = place.feature(step)
        core_in[step].wait_recv()
        go_right.wait_recv()
        slot = 2 * (4 - step) - 1
        if step == 3:
            tok_send[slot, 0] = add(own_tok[f, 0], from_core[f, 0], right_far[...]).astype(BF16)
            tok_send[slot, 1] = add(own_tok[f, 1], from_core[f, 1]).astype(BF16)
        else:
            tok_send[slot] = add(own_tok[f], from_core[f], right_in[2 - step]).astype(BF16)
        go_right = go(tok_send.at[slot], right_in.at[3 - step], place.along_z(1))
        f = place.feature(-step)
        core_in[-step].wait_recv()
        go_left.wait_recv()
        if step == 3:
            tok_send[slot + 1, 0] = add(own_tok[f, 0], from_core[f, 0]).astype(BF16)
            tok_send[slot + 1, 1] = add(own_tok[f, 1], from_core[f, 1], left_far[...]).astype(BF16)
        else:
            tok_send[slot + 1] = add(own_tok[f], from_core[f], left_in[2 - step]).astype(BF16)
        go_left = go(tok_send.at[slot + 1], left_in.at[3 - step], place.along_z(-1))

    pass_on(3)

    def up_more(index, carry):
        up_tile(tile_at(1, 1 - index))
        down_tile(tile_at(-1, 1 - index))
        return carry

    lax.fori_loop(0, 2, up_more, 0)
    up_right, down_left = [None, None], [None, None]
    for side in (1, 0):
        far_in[0][side].wait_recv()
        y_send[0, side] = add(part[0, tile_at(1, side)], y_far[0, side]).astype(BF16)
        up_right[side] = go(y_send.at[0, side], y_right.at[0, side], right)
        far_in[1][side].wait_recv()
        y_send[1, side] = add(part[1, tile_at(-1, side)], y_far[1, side]).astype(BF16)
        down_left[side] = go(y_send.at[1, side], y_left.at[1, side], left)

    tok_features(5, (1, -1, 0), lambda index: 1 + 6 * index - (index // 2) * 5)
    pass_on(2)

    def own_tiles(index, carry):
        up_tile(tile_at(0, 1 - index))
        down_tile(tile_at(0, 1 - index))
        return carry

    lax.fori_loop(0, 2, own_tiles, 0)
    pass_on(1)

    hi = []
    up_left[1].wait_recv()
    up_right[1].wait_recv()
    hi_out[0] = add(part[0, twin], y_left[0, 1], y_right[0, 1]).astype(BF16)
    hi.append(go(hi_out.at[0], hi_in.at[0], place.partner_hi()))
    down_left[1].wait_recv()
    down_right[1].wait_recv()
    hi_out[1] = add(part[1, twin], y_left[1, 1], y_right[1, 1]).astype(BF16)
    hi.append(go(hi_out.at[1], hi_in.at[1], place.partner_hi()))

    f = place.f
    core_in[0].wait_recv()
    go_right.wait_recv()
    go_left.wait_recv()
    other = 1 - xl
    lo_out[...] = add(own_tok[f, other], from_core[f, other], right_in[2, other], left_in[2, other]).astype(BF16)
    lo = go(lo_out, lo_in, place.partner_lo())
    lo.wait_recv()
    home[...] = add(own_tok[f, xl], from_core[f, xl], right_in[2, xl], left_in[2, xl], lo_in[...]).astype(BF16)
    back = go(home, tok_out, place.back_to())

    for which, outputs, first, second in ((0, up_out, up_left, up_right), (1, down_out, down_left, down_right)):
        first[0].wait_recv()
        second[0].wait_recv()
        hi[which].wait_recv()
        outputs[...] = add(part[which, mine], y_left[which, 0], y_right[which, 0], hi_in[which])
    back.wait_recv()
    copies.finish()


COPIES = 93


def vmem(count):
    return [pl.BlockSpec(memory_space=pltpu.VMEM)] * count


def sds(shape, dtype=BF16):
    return jax.ShapeDtypeStruct(shape, dtype)


def offsets(up_layout, up_counts, down_layout, down_counts):
    up_ids, down_ids = up_layout[0, 0], down_layout[0, 0]
    ids = jnp.stack([up_ids, (down_ids % NB) * NB + down_ids // NB])
    counts = jnp.stack([up_counts[0, 0], down_counts[0, 0]])
    numbers = jnp.arange(128, dtype=jnp.int32)
    slots = numbers[:CAP]
    hit = (ids[:, :, None] == numbers) & (slots[None, :] < counts[:, None])[:, :, None]
    slot_of = CAP + jnp.sum(jnp.where(hit, slots[None, :, None] - CAP, 0), axis=1)
    place = ((slot_of + numbers % NB) % 2) * SHIFT + slot_of // 2
    row, lane = ids // NB, ids % NB
    take = ((lane + slots) % 2) * SLAB + (lane // 2) * NB + row
    take = jnp.pad(take, ((0, 0), (0, 128 - CAP)))
    return jnp.concatenate([place, take, jnp.zeros((4, 128), jnp.int32)], axis=0)


def body(tokens, up_blocks, up_layout, up_counts, down_blocks, down_layout, down_counts, grad_out):
    pay = jnp.stack([up_blocks[0, 0], down_blocks[0, 0]]).reshape(2, PAIRS, 2, BLOCK, BLOCK)
    pay = pay.transpose(0, 1, 3, 2, 4).reshape(2, ROWS, 2 * BLOCK)
    meta = offsets(up_layout, up_counts, down_layout, down_counts)
    tile = (ROWS, 128)
    piece = (TOK, FEAT)
    tok_grad, up_sum, down_sum = pl.pallas_call(
        kernel,
        out_shape=(sds(piece), sds(tile, F32), sds(tile, F32)),
        in_specs=vmem(4),
        out_specs=tuple(vmem(3)),
        scratch_shapes=[
            pltpu.VMEM((2, 8, 2, 2) + piece, BF16),
            pltpu.VMEM((2, 8) + tile, BF16),
            pltpu.VMEM((8, 8, 128), jnp.int32),
            pltpu.SMEM((8, 8, 128), jnp.int32),
            pltpu.VMEM((2, 8, FEAT, FEAT), BF16),
            pltpu.VMEM((2 * SHIFT, BLOCK, 128), BF16),
            pltpu.VMEM((GROUP, FEAT), F32),
            pltpu.VMEM((GROUP, FEAT), F32),
            pltpu.VMEM((GROUP, FEAT), BF16),
            pltpu.VMEM((GROUP, FEAT), BF16),
            pltpu.VMEM((2 * SLAB, BLOCK, 128), BF16),
            pltpu.VMEM((8, 2) + piece, F32),
            pltpu.VMEM((8, 2) + piece, BF16),
            pltpu.VMEM((8, 2) + piece, BF16),
            pltpu.VMEM((7, 2) + piece, BF16),
            pltpu.VMEM((3, 2) + piece, BF16),
            pltpu.VMEM((3, 2) + piece, BF16),
            pltpu.VMEM(piece, BF16),
            pltpu.VMEM(piece, BF16),
            pltpu.VMEM(piece, BF16),
            pltpu.VMEM(piece, BF16),
            pltpu.VMEM(piece, BF16),
            pltpu.VMEM((2, 8) + tile, BF16),
            pltpu.VMEM((2, 2) + tile, BF16),
            pltpu.VMEM((2, 2) + tile, BF16),
            pltpu.VMEM((2, 2) + tile, BF16),
            pltpu.VMEM((2, 2) + tile, BF16),
            pltpu.VMEM((2,) + tile, BF16),
            pltpu.VMEM((2,) + tile, BF16),
            pltpu.SemaphoreType.DMA((8,)),
            pltpu.SemaphoreType.DMA((COPIES,)),
            pltpu.SemaphoreType.DMA((COPIES,)),
        ],
        compiler_params=pltpu.CompilerParams(collective_id=0, has_side_effects=True, vmem_limit_bytes=60 * 2**20),
        name="layer",
    )(tokens, grad_out, pay, meta)

    def slots(total, counts):
        flat = total.reshape(PAIRS, BLOCK, 2, BLOCK).transpose(0, 2, 1, 3).reshape(CAP, BLOCK * BLOCK)
        live = jnp.arange(CAP, dtype=jnp.int32) < counts[0, 0]
        return jnp.where(live[:, None], flat, 0.0)[None, None]

    return tok_grad, slots(up_sum, up_counts), slots(down_sum, down_counts)


def solution(mesh):
    in_specs = (
        P("col", "row"),
        P("row", "col", None, None),
        P("row", "col", None),
        P("row", "col"),
        P("row", "col", None, None),
        P("row", "col", None),
        P("row", "col"),
        P("col", "row"),
    )
    out_specs = (P("col", "row"), P("row", "col", None, None), P("row", "col", None, None))
    return jax.shard_map(body, mesh=mesh, in_specs=in_specs, out_specs=out_specs, check_vma=False)
```

```python
import jax
import jax.numpy as jnp
from jax import lax
from jax.experimental import pallas as pl
from jax.experimental.pallas import tpu as pltpu
from jax.sharding import PartitionSpec as P

BLOCK = 64
CAP = 30
PAIRS = CAP // 2
NB = 10
ROWS = PAIRS * BLOCK
EXTRA = 16
TOK = 96
FEAT = NB * BLOCK
GROUP = 4 * TOK
SHIFT = 16
SLAB = 5 * NB
MESH = pl.DeviceIdType.MESH
BF16 = jnp.bfloat16
F32 = jnp.float32

GELU_C = 0.7978845608028654
GELU_A = 0.044715


class Place:
    def __init__(self):
        self.p = lax.axis_index("row")
        col = lax.axis_index("col")
        self.z, self.xl, self.core = col // 4, (col // 2) % 2, col % 2
        self.y, self.xh = self.p // 2, self.p % 2
        self.f = (self.z + 7) % 8

    def col(self, z, xl, core):
        return z * 4 + xl * 2 + core

    def sibling(self):
        return (self.p, self.col(self.z, self.xl, 1 - self.core))

    def partner_lo(self):
        return (self.p, self.col(self.z, 1 - self.xl, self.core))

    def partner_hi(self):
        return (self.y * 2 + 1 - self.xh, self.col(self.z, self.xl, self.core))

    def along_y(self, step):
        return (((self.y + step + 4) % 4) * 2 + self.xh, self.col(self.z, self.xl, self.core))

    def along_z(self, step):
        return (self.p, self.col((self.z + step + 8) % 8, self.xl, self.core))

    def out_to(self):
        return ((self.z + 4 * self.core) % 8, self.col((self.p + 1) % 8, self.xl, self.core))

    def back_to(self):
        return (self.f, self.col((self.p + 8 - 4 * self.core) % 8, self.xl, self.core))

    def feature(self, step):
        return (self.z + step + 7 + 8) % 8


class Copies:
    def __init__(self, send_sems, recv_sems):
        self.send_sems, self.recv_sems = send_sems, recv_sems
        self.number = 0
        self.made = []

    def reserve(self, count):
        first = self.number
        self.number += count
        return first

    def copy(self, src, dst, device, index):
        return pltpu.make_async_remote_copy(
            src_ref=src,
            dst_ref=dst,
            send_sem=self.send_sems.at[index],
            recv_sem=self.recv_sems.at[index],
            device_id=device,
            device_id_type=MESH,
        )

    def start(self, src, dst, device):
        copy = self.copy(src, dst, device, self.reserve(1))
        copy.start()
        self.made.append(copy)
        return copy

    def started(self, src, dst, device, index):
        copy = self.copy(src, dst, device, index)
        self.made.append(copy)
        return copy

    def finish(self):
        for copy in self.made:
            copy.wait_send()


def greet(place):
    devices = [
        place.sibling(),
        place.partner_lo(),
        place.partner_hi(),
        place.along_y(1),
        place.along_y(-1),
        place.along_y(2),
        place.along_z(1),
        place.along_z(-1),
        place.out_to(),
        place.back_to(),
    ]
    barrier = pltpu.get_barrier_semaphore()
    for device in devices:
        pl.semaphore_signal(barrier, inc=1, device_id=device, device_id_type=MESH)
    return barrier, len(devices)


def add(*parts):
    total = parts[0].astype(F32)
    for part in parts[1:]:
        total = total + part.astype(F32)
    return total


def kernel(
    tok, out, meta, up_blocks, up_counts, down_blocks, down_counts,
    tok_out, up_out, down_out,
    pay, wide, pairs,
    held, strip, numbers, numbers_sm, dense, blocks, pre, slope_part, hidden, pre_grad, grads,
    own_tok, core_send, from_core, tok_send, right_in, left_in, right_far, left_far, lo_out, lo_in, home,
    part, x_in, y_far, y_right, y_left, y_send, hi_out, hi_in,
    meta_sems, send_sems, recv_sems,
):
    place = Place()
    z, y, xh, xl, core = place.z, place.y, place.xh, place.xl, place.core
    mine, twin = place.p, y * 2 + 1 - xh
    right, left = place.along_y(1), place.along_y(-1)
    barrier, greetings = greet(place)

    for which, raw in enumerate((up_blocks, down_blocks)):
        for k in range(BLOCK // 2):
            wide[k, 0:CAP, :] = raw[0, 0, :, k * 128 : (k + 1) * 128].astype(F32)
            even = wide[k, pl.ds(0, PAIRS, stride=2), :]
            odd = wide[k, pl.ds(1, PAIRS, stride=2), :]
            pairs[:, 2 * k, :] = jnp.concatenate([even[:, :BLOCK], odd[:, :BLOCK]], axis=1)
            pairs[:, 2 * k + 1, :] = jnp.concatenate([even[:, BLOCK:], odd[:, BLOCK:]], axis=1)
        pay[which] = pairs[...].reshape(ROWS, 128).astype(BF16)

    pl.semaphore_wait(barrier, greetings)
    copies = Copies(send_sems, recv_sems)
    go = copies.start

    def along_y(numbers_ref, tile_ref, tile):
        return [
            (go(numbers_ref, numbers.at[tile], device), go(tile_ref, strip.at[:, tile], device))
            for device in (right, left, place.along_y(2))
        ]

    perm_tok = go(tok, held.at[0, place.p, core, xl], place.out_to())
    def to_scalars(source, tile, index):
        copy = pltpu.make_async_copy(source, numbers_sm.at[tile], meta_sems.at[index])
        copy.start()
        return copy

    def fill(which, tile, data):
        turned = jnp.concatenate([data[:, BLOCK:], data[:, :BLOCK]], axis=1)
        blocks[0:PAIRS] = data.reshape(PAIRS, BLOCK, 128)
        blocks[SHIFT : SHIFT + PAIRS] = turned.reshape(PAIRS, BLOCK, 128)
        for i in range(NB):
            for j in range(NB):
                half = (j % 2) * BLOCK
                dense[which, tile, i * BLOCK : (i + 1) * BLOCK, j * BLOCK : (j + 1) * BLOCK] = blocks[
                    numbers_sm[tile, which, i * NB + j], :, half : half + BLOCK
                ]

    def fill_tiles(tiles):
        def step(index, carry):
            which, tile = index % 2, tiles(index // 2)
            fill(which, tile, strip[which, tile])
            return carry

        return step

    zeros = jnp.zeros((BLOCK, 128), BF16)
    blocks[PAIRS] = zeros
    blocks[SHIFT + PAIRS] = zeros
    pre[...] = jnp.zeros_like(pre)
    slope_part[...] = jnp.zeros_like(slope_part)
    to_scalars(meta, mine, 0).wait()

    def fill_mine(which, carry):
        fill(which, mine, pay[which])
        return carry

    lax.fori_loop(0, 2, fill_mine, 0)

    def toks(step):
        return held.at[0, place.feature(step), core]

    def outs(step):
        return held.at[1, place.feature(step), core, xl]

    def both_outs(step):
        return held.at[1, place.feature(step), core]

    def to_core(ref):
        return go(ref, ref, place.sibling())

    lo_outs, core_toks, core_outs = {}, {}, {}

    def tile_at(step, side):
        return ((y + step + 4) % 4) * 2 + (xh + side) % 2

    def multiply(step):
        f = place.feature(step)
        t = held[0, f].reshape(GROUP, FEAT)
        pre[...] += jnp.dot(t, dense[0, f], preferred_element_type=F32)
        g = held[1, f].reshape(GROUP, FEAT)
        slope_part[...] += lax.dot_general(g, dense[1, f], (((1,), (1,)), ((), ())), preferred_element_type=F32)

    def multiply_ready(steps):
        for step in steps:
            core_toks[step].wait_recv()
            core_outs[step].wait_recv()

    perm_tok.wait_recv()
    piece = held.at[0, place.f, core, xl]
    lo_tok = go(piece, piece, place.partner_lo())
    swap_meta = go(meta, numbers.at[mine], place.partner_hi())
    swap = go(pay, strip.at[:, mine], place.partner_hi())

    lo_tok.wait_recv()
    right_tok = go(toks(0), toks(0), place.along_z(1))
    left_tok = go(toks(0), toks(0), place.along_z(-1))
    core_toks[0] = to_core(toks(0))
    perm_out = go(out, held.at[1, place.p, core, xl], place.out_to())
    y_own = along_y(meta, pay, mine)

    swap_meta.wait_recv()
    twin_scalars = to_scalars(numbers.at[twin], twin, 1)
    swap.wait_recv()
    y_twin = along_y(numbers.at[twin], strip.at[:, twin], twin)
    twin_scalars.wait()

    def tok_step(step):
        nonlocal right_tok, left_tok
        right_tok.wait_recv()
        ref = toks(-step)
        if step < 4:
            right_tok = go(ref, ref, place.along_z(1))
        core_toks[4 if step == 4 else -step] = to_core(ref)
        if step < 4:
            left_tok.wait_recv()
            ref = toks(step)
            if step < 3:
                left_tok = go(ref, ref, place.along_z(-1))
            core_toks[step] = to_core(ref)

    def out_step(step):
        nonlocal right_out, left_out
        if step < 4:
            right_out.wait_recv()
            ref = outs(-step)
            if step < 3:
                right_out = go(ref, ref, place.along_z(1))
            lo_outs[-step] = go(ref, ref, place.partner_lo())
        left_out.wait_recv()
        ref = outs(step)
        if step < 4:
            left_out = go(ref, ref, place.along_z(-1))
        lo_outs[step] = go(ref, ref, place.partner_lo())

    def outs_to_core(steps):
        for step in steps:
            lo_outs[step].wait_recv()
            core_outs[step] = to_core(both_outs(step))

    def out_begin():
        perm_out.wait_recv()
        lo_outs[0] = go(outs(0), outs(0), place.partner_lo())
        return go(outs(0), outs(0), place.along_z(1)), go(outs(0), outs(0), place.along_z(-1))

    def tiles_came(came, side, first):
        scalars = []
        for number, step in enumerate((-1, 1, 2)):
            came[number][0].wait_recv()
            scalars.append(to_scalars(numbers.at[tile_at(step, side)], tile_at(step, side), first + number))
        for number in range(3):
            came[number][1].wait_recv()
            scalars[number].wait()

    def fill_along_y(side):
        lax.fori_loop(0, 6, fill_tiles(lambda index: tile_at(index + 1, side)), 0)

    tok_step(1)
    lax.fori_loop(0, 2, fill_tiles(lambda index: twin), 0)
    right_out, left_out = out_begin()
    tok_step(2)
    out_step(1)
    outs_to_core((0,))
    tok_step(3)
    out_step(2)
    outs_to_core((-1, 1))
    tok_step(4)
    out_step(3)
    outs_to_core((-2, 2))
    tiles_came(y_own, 0, 2)
    fill_along_y(0)
    out_step(4)
    outs_to_core((-3, 3))
    tiles_came(y_twin, 1, 5)
    fill_along_y(1)
    multiply_ready((0, -1, 1))

    def near_features(index, carry):
        multiply(index - 1)
        return carry

    lax.fori_loop(0, 3, near_features, 0)
    outs_to_core((4,))
    multiply_ready((-2, 2, -3, 3))

    def late_features(index, carry):
        multiply(2 + index + index // 2)
        return carry

    lax.fori_loop(0, 4, late_features, 0)
    multiply_ready((4,))
    multiply(4)

    def activate(index, carry):
        rows = pl.ds(pl.multiple_of(index * 32, 32), 32)
        v = pre[rows, :]
        t = jnp.tanh(GELU_C * (v + GELU_A * v * v * v))
        hidden[rows, :] = (0.5 * v * (1.0 + t)).astype(BF16)
        slope = 0.5 * (1.0 + t) + 0.5 * v * (1.0 - t * t) * GELU_C * (1.0 + 3.0 * GELU_A * v * v)
        pre_grad[rows, :] = (slope_part[rows, :] * slope).astype(BF16)
        return carry

    lax.fori_loop(0, GROUP // 32, activate, 0)

    def extract(product, which, tile):
        product = product.astype(BF16)
        for slab in range(5):
            data = product[:, slab * 128 : (slab + 1) * 128]
            turned = jnp.concatenate([data[:, BLOCK:], data[:, :BLOCK]], axis=1)
            grads[slab * NB : (slab + 1) * NB] = data.reshape(NB, BLOCK, 128)
            grads[SLAB + slab * NB : SLAB + (slab + 1) * NB] = turned.reshape(NB, BLOCK, 128)
        for slot in range(CAP):
            half = (slot % 2) * BLOCK
            at = (slot // 2) * BLOCK
            part[which, tile, at : at + BLOCK, half : half + BLOCK] = grads[
                numbers_sm[tile, 2 + which, slot], :, half : half + BLOCK
            ]

    def up_tile(tile):
        left_side = held[0, tile].reshape(GROUP, FEAT)
        extract(
            lax.dot_general(left_side, pre_grad[...], (((0,), (0,)), ((), ())), preferred_element_type=F32), 0, tile
        )

    def down_tile(tile):
        right_side = held[1, tile].reshape(GROUP, FEAT)
        extract(
            lax.dot_general(hidden[...], right_side, (((0,), (0,)), ((), ())), preferred_element_type=F32), 1, tile
        )

    half_rows = GROUP // 2

    def tok_feature(f, index):
        def rows_of(which_core):
            rows = pre_grad[pl.ds(pl.multiple_of(which_core * half_rows, half_rows), half_rows), :]
            return lax.dot_general(rows, dense[0, f], (((1,), (1,)), ((), ())), preferred_element_type=F32)

        core_send[f] = rows_of(1 - core).astype(BF16).reshape(2, TOK, FEAT)
        copies.copy(core_send.at[f], from_core.at[f], place.sibling(), index).start()
        own_tok[f] = rows_of(core).reshape(2, TOK, FEAT)

    core_first = copies.reserve(8)
    core_in = {}

    def tok_features(first, steps, step_of):
        def one(index, carry):
            tok_feature(place.feature(step_of(index)), core_first + first + index)
            return carry

        lax.fori_loop(0, len(steps), one, 0)
        for number, step in enumerate(steps):
            f = place.feature(step)
            core_in[step] = copies.started(
                core_send.at[f], from_core.at[f], place.sibling(), core_first + first + number
            )

    x_steps = (2, 1, -1, 0)
    x_first = copies.reserve(4)
    far_first = copies.reserve(2)
    near_first = copies.reserve(2)

    def x_send(slot, tile):
        up_tile(tile)
        copies.copy(part.at[0, tile], x_in.at[slot], place.partner_hi(), x_first + slot).start()

    def early_tiles(index, carry):
        x_send(index, tile_at(2 - index, 1))
        tile = tile_at(2, 1 - index)
        down_tile(tile)
        copies.copy(part.at[1, tile], y_far.at[1, 1 - index], left, far_first + index).start()
        return carry

    def next_tiles(index, carry):
        x_send(2 + index, tile_at(index - 1, 1))
        tile = tile_at(1, 1 - index)
        down_tile(tile)
        copies.copy(part.at[1, tile], y_right.at[1, 1 - index], right, near_first + index).start()
        return carry

    tok_features(0, (4, 3, -3), lambda index: 4 - index + (index // 2) * 3)
    lax.fori_loop(0, 2, early_tiles, 0)
    far_down = [
        copies.started(part.at[1, tile_at(2, side)], y_far.at[1, side], left, far_first + 1 - side) for side in range(2)
    ]

    f = place.feature(4)
    core_in[4].wait_recv()
    tok_send[0] = add(own_tok[f], from_core[f]).astype(BF16)
    go_right = go(tok_send.at[0, 0], right_far, place.along_z(1))
    go_left = go(tok_send.at[0, 1], left_far, place.along_z(-1))

    lax.fori_loop(0, 2, next_tiles, 0)
    down_right = [
        copies.started(part.at[1, tile_at(1, side)], y_right.at[1, side], right, near_first + 1 - side) for side in range(2)
    ]
    from_twin = {
        step: copies.started(part.at[0, tile_at(step, 1)], x_in.at[slot], place.partner_hi(), x_first + slot)
        for slot, step in enumerate(x_steps)
    }

    def pass_on(step):
        nonlocal go_right, go_left
        f = place.feature(step)
        core_in[step].wait_recv()
        go_right.wait_recv()
        slot = 2 * (4 - step) - 1
        if step == 3:
            tok_send[slot, 0] = add(own_tok[f, 0], from_core[f, 0], right_far[...]).astype(BF16)
            tok_send[slot, 1] = add(own_tok[f, 1], from_core[f, 1]).astype(BF16)
        else:
            tok_send[slot] = add(own_tok[f], from_core[f], right_in[2 - step]).astype(BF16)
        go_right = go(tok_send.at[slot], right_in.at[3 - step], place.along_z(1))
        f = place.feature(-step)
        core_in[-step].wait_recv()
        go_left.wait_recv()
        if step == 3:
            tok_send[slot + 1, 0] = add(own_tok[f, 0], from_core[f, 0]).astype(BF16)
            tok_send[slot + 1, 1] = add(own_tok[f, 1], from_core[f, 1], left_far[...]).astype(BF16)
        else:
            tok_send[slot + 1] = add(own_tok[f], from_core[f], left_in[2 - step]).astype(BF16)
        go_left = go(tok_send.at[slot + 1], left_in.at[3 - step], place.along_z(-1))

    pass_on(3)
    tok_features(3, (2, -2), lambda index: 2 + 4 * index)

    def more_tiles(index, carry):
        up_tile(tile_at(2 + index, 0))
        down_tile(tile_at(-1, 1 - index))
        return carry

    lax.fori_loop(0, 2, more_tiles, 0)
    from_twin[2].wait_recv()
    y_send[0, 0] = add(part[0, tile_at(2, 0)], x_in[0]).astype(BF16)
    far_up = go(y_send.at[0, 0], y_far.at[0, 0], right)
    down_left = [None, None]
    for side in (1, 0):
        far_down[side].wait_recv()
        y_send[1, side] = add(part[1, tile_at(-1, side)], y_far[1, side]).astype(BF16)
        down_left[side] = go(y_send.at[1, side], y_left.at[1, side], left)
    pass_on(2)
    from_twin[-1].wait_recv()
    y_send[0, 1] = add(part[0, tile_at(-1, 0)], x_in[2]).astype(BF16)
    up_left = go(y_send.at[0, 1], y_left.at[0, 0], left)

    tok_features(5, (1, -1, 0), lambda index: 1 + 6 * index - (index // 2) * 5)

    def last_tiles(index, carry):
        up_tile(tile_at(1 - index, 0))
        down_tile(tile_at(0, 1 - index))
        return carry

    lax.fori_loop(0, 2, last_tiles, 0)
    from_twin[1].wait_recv()
    far_up.wait_recv()
    y_send[0, 2] = add(part[0, tile_at(1, 0)], x_in[1], y_far[0, 0]).astype(BF16)
    up_right = go(y_send.at[0, 2], y_right.at[0, 0], right)
    pass_on(1)

    down_left[1].wait_recv()
    down_right[1].wait_recv()
    hi_out[...] = add(part[1, twin], y_left[1, 1], y_right[1, 1]).astype(BF16)
    hi = go(hi_out, hi_in, place.partner_hi())

    def put(target, total, counts):
        pairs[...] = total.reshape(PAIRS, BLOCK, 128)
        slot = 2 * lax.broadcasted_iota(jnp.int32, (PAIRS, 128), 0)
        even_live, odd_live = slot < counts[0, 0], slot + 1 < counts[0, 0]
        for k in range(BLOCK // 2):
            low, high = pairs[:, 2 * k, :], pairs[:, 2 * k + 1, :]
            even = jnp.concatenate([low[:, :BLOCK], high[:, :BLOCK]], axis=1)
            odd = jnp.concatenate([low[:, BLOCK:], high[:, BLOCK:]], axis=1)
            wide[k, pl.ds(0, PAIRS, stride=2), :] = jnp.where(even_live, even, 0.0)
            wide[k, pl.ds(1, PAIRS, stride=2), :] = jnp.where(odd_live, odd, 0.0)
            target[0, 0, :, k * 128 : (k + 1) * 128] = wide[k, 0:CAP, :]

    from_twin[0].wait_recv()
    up_left.wait_recv()
    up_right.wait_recv()
    put(up_out, add(part[0, mine], x_in[3], y_left[0, 0], y_right[0, 0]), up_counts)

    f = place.f
    core_in[0].wait_recv()
    go_right.wait_recv()
    go_left.wait_recv()
    other = 1 - xl
    lo_out[...] = add(own_tok[f, other], from_core[f, other], right_in[2, other], left_in[2, other]).astype(BF16)
    lo = go(lo_out, lo_in, place.partner_lo())

    down_left[0].wait_recv()
    down_right[0].wait_recv()
    lo.wait_recv()
    home[...] = add(own_tok[f, xl], from_core[f, xl], right_in[2, xl], left_in[2, xl], lo_in[...]).astype(BF16)
    back = go(home, tok_out, place.back_to())

    hi.wait_recv()
    put(down_out, add(part[1, mine], y_left[1, 0], y_right[1, 0], hi_in[...]), down_counts)
    back.wait_recv()
    copies.finish()
    assert copies.number == COPIES, copies.number


COPIES = 87


def vmem(count):
    return [pl.BlockSpec(memory_space=pltpu.VMEM)] * count


def sds(shape, dtype=BF16):
    return jax.ShapeDtypeStruct(shape, dtype)


def offsets(up_layout, up_counts, down_layout, down_counts):
    up_ids, down_ids = up_layout[0, 0], down_layout[0, 0]
    ids = jnp.stack([up_ids, (down_ids % NB) * NB + down_ids // NB])
    counts = jnp.stack([up_counts[0, 0], down_counts[0, 0]])
    numbers = jnp.arange(128, dtype=jnp.int32)
    slots = numbers[:CAP]
    hit = (ids[:, :, None] == numbers) & (slots[None, :] < counts[:, None])[:, :, None]
    slot_of = CAP + jnp.sum(jnp.where(hit, slots[None, :, None] - CAP, 0), axis=1)
    place = ((slot_of + numbers % NB) % 2) * SHIFT + slot_of // 2
    row, lane = ids // NB, ids % NB
    take = ((lane + slots) % 2) * SLAB + (lane // 2) * NB + row
    take = jnp.pad(take, ((0, 0), (0, 128 - CAP)))
    return jnp.concatenate([place, take, jnp.zeros((4, 128), jnp.int32)], axis=0)


def body(tokens, up_blocks, up_layout, up_counts, down_blocks, down_layout, down_counts, grad_out):
    meta = offsets(up_layout, up_counts, down_layout, down_counts)
    tile = (ROWS, 128)
    scalar = [pl.BlockSpec(memory_space=pltpu.SMEM)]
    piece = (TOK, FEAT)
    return pl.pallas_call(
        kernel,
        out_shape=(sds(piece), sds((1, 1, CAP, BLOCK * BLOCK), F32), sds((1, 1, CAP, BLOCK * BLOCK), F32)),
        in_specs=vmem(4) + scalar + vmem(1) + scalar,
        out_specs=tuple(vmem(3)),
        scratch_shapes=[
            pltpu.VMEM((2,) + tile, BF16),
            pltpu.VMEM((BLOCK // 2, CAP + 2, 128), F32),
            pltpu.VMEM((PAIRS, BLOCK, 128), F32),
            pltpu.VMEM((2, 8, 2, 2) + piece, BF16),
            pltpu.VMEM((2, 8) + tile, BF16),
            pltpu.VMEM((8, 8, 128), jnp.int32),
            pltpu.SMEM((8, 8, 128), jnp.int32),
            pltpu.VMEM((2, 8, FEAT, FEAT), BF16),
            pltpu.VMEM((2 * SHIFT, BLOCK, 128), BF16),
            pltpu.VMEM((GROUP, FEAT), F32),
            pltpu.VMEM((GROUP, FEAT), F32),
            pltpu.VMEM((GROUP, FEAT), BF16),
            pltpu.VMEM((GROUP, FEAT), BF16),
            pltpu.VMEM((2 * SLAB, BLOCK, 128), BF16),
            pltpu.VMEM((8, 2) + piece, F32),
            pltpu.VMEM((8, 2) + piece, BF16),
            pltpu.VMEM((8, 2) + piece, BF16),
            pltpu.VMEM((7, 2) + piece, BF16),
            pltpu.VMEM((3, 2) + piece, BF16),
            pltpu.VMEM((3, 2) + piece, BF16),
            pltpu.VMEM(piece, BF16),
            pltpu.VMEM(piece, BF16),
            pltpu.VMEM(piece, BF16),
            pltpu.VMEM(piece, BF16),
            pltpu.VMEM(piece, BF16),
            pltpu.VMEM((2, 8) + tile, BF16),
            pltpu.VMEM((4,) + tile, BF16),
            pltpu.VMEM((2, 2) + tile, BF16),
            pltpu.VMEM((2, 2) + tile, BF16),
            pltpu.VMEM((2, 2) + tile, BF16),
            pltpu.VMEM((2, 3) + tile, BF16),
            pltpu.VMEM(tile, BF16),
            pltpu.VMEM(tile, BF16),
            pltpu.SemaphoreType.DMA((8,)),
            pltpu.SemaphoreType.DMA((COPIES,)),
            pltpu.SemaphoreType.DMA((COPIES,)),
        ],
        compiler_params=pltpu.CompilerParams(collective_id=0, has_side_effects=True, vmem_limit_bytes=60 * 2**20),
        name="layer",
    )(tokens, grad_out, meta, up_blocks, up_counts, down_blocks, down_counts)


def solution(mesh):
    in_specs = (
        P("col", "row"),
        P("row", "col", None, None),
        P("row", "col", None),
        P("row", "col"),
        P("row", "col", None, None),
        P("row", "col", None),
        P("row", "col"),
        P("col", "row"),
    )
    out_specs = (P("col", "row"), P("row", "col", None, None), P("row", "col", None, None))
    return jax.shard_map(body, mesh=mesh, in_specs=in_specs, out_specs=out_specs, check_vma=False)
```

```python
import jax
import jax.numpy as jnp
from jax import lax
from jax.experimental import pallas as pl
from jax.experimental.pallas import tpu as pltpu
from jax.sharding import PartitionSpec as P

BLOCK = 64
CAP = 30
PAIRS = CAP // 2
NB = 10
ROWS = PAIRS * BLOCK
EXTRA = 16
TOK = 96
FEAT = NB * BLOCK
GROUP = 4 * TOK
SHIFT = 16
SLAB = 5 * NB
MESH = pl.DeviceIdType.MESH
BF16 = jnp.bfloat16
F32 = jnp.float32

GELU_C = 0.7978845608028654
GELU_A = 0.044715


class Place:
    def __init__(self):
        self.p = lax.axis_index("row")
        col = lax.axis_index("col")
        self.z, self.xl, self.core = col // 4, (col // 2) % 2, col % 2
        self.y, self.xh = self.p // 2, self.p % 2
        self.f = (self.z + 7) % 8

    def col(self, z, xl, core):
        return z * 4 + xl * 2 + core

    def sibling(self):
        return (self.p, self.col(self.z, self.xl, 1 - self.core))

    def partner_lo(self):
        return (self.p, self.col(self.z, 1 - self.xl, self.core))

    def partner_hi(self):
        return (self.y * 2 + 1 - self.xh, self.col(self.z, self.xl, self.core))

    def along_y(self, step):
        return (((self.y + step + 4) % 4) * 2 + self.xh, self.col(self.z, self.xl, self.core))

    def along_z(self, step):
        return (self.p, self.col((self.z + step + 8) % 8, self.xl, self.core))

    def out_to(self):
        return ((self.z + 4 * self.core) % 8, self.col((self.p + 1) % 8, self.xl, self.core))

    def back_to(self):
        return (self.f, self.col((self.p + 8 - 4 * self.core) % 8, self.xl, self.core))

    def feature(self, step):
        return (self.z + step + 7 + 8) % 8


class Copies:
    def __init__(self, send_sems, recv_sems):
        self.send_sems, self.recv_sems = send_sems, recv_sems
        self.number = 0
        self.made = []

    def reserve(self, count):
        first = self.number
        self.number += count
        return first

    def copy(self, src, dst, device, index):
        return pltpu.make_async_remote_copy(
            src_ref=src,
            dst_ref=dst,
            send_sem=self.send_sems.at[index],
            recv_sem=self.recv_sems.at[index],
            device_id=device,
            device_id_type=MESH,
        )

    def start(self, src, dst, device):
        copy = self.copy(src, dst, device, self.reserve(1))
        copy.start()
        self.made.append(copy)
        return copy

    def started(self, src, dst, device, index):
        copy = self.copy(src, dst, device, index)
        self.made.append(copy)
        return copy

    def finish(self):
        for copy in self.made:
            copy.wait_send()


def greet(place):
    devices = [
        place.sibling(),
        place.partner_lo(),
        place.partner_hi(),
        place.along_y(1),
        place.along_y(-1),
        place.along_y(2),
        place.along_z(1),
        place.along_z(-1),
        place.out_to(),
        place.back_to(),
    ]
    barrier = pltpu.get_barrier_semaphore()
    for device in devices:
        pl.semaphore_signal(barrier, inc=1, device_id=device, device_id_type=MESH)
    return barrier, len(devices)


def add(*parts):
    total = parts[0].astype(F32)
    for part in parts[1:]:
        total = total + part.astype(F32)
    return total


def kernel(
    tok, out, meta, up_blocks, up_counts, down_blocks, down_counts,
    tok_out, up_out, down_out,
    pay, wide, pairs,
    held, strip, numbers, numbers_sm, dense, blocks, pre, slope_part, hidden, pre_grad, grads,
    own_tok, core_send, from_core, tok_send, right_in, left_in, right_far, left_far, lo_out, lo_in, home,
    part, x_in, y_far, y_right, y_left, y_send, hi_out, hi_in,
    meta_sems, send_sems, recv_sems,
):
    place = Place()
    z, y, xh, xl, core = place.z, place.y, place.xh, place.xl, place.core
    mine, twin = place.p, y * 2 + 1 - xh
    right, left = place.along_y(1), place.along_y(-1)
    barrier, greetings = greet(place)

    for which, raw in enumerate((up_blocks, down_blocks)):
        for k in range(BLOCK // 2):
            wide[k, 0:CAP, :] = raw[0, 0, :, k * 128 : (k + 1) * 128].astype(F32)
            even = wide[k, pl.ds(0, PAIRS, stride=2), :]
            odd = wide[k, pl.ds(1, PAIRS, stride=2), :]
            pairs[:, 2 * k, :] = jnp.concatenate([even[:, :BLOCK], odd[:, :BLOCK]], axis=1)
            pairs[:, 2 * k + 1, :] = jnp.concatenate([even[:, BLOCK:], odd[:, BLOCK:]], axis=1)
        pay[which] = pairs[...].reshape(ROWS, 128).astype(BF16)

    pl.semaphore_wait(barrier, greetings)
    copies = Copies(send_sems, recv_sems)
    go = copies.start

    def along_y(numbers_ref, tile_ref, tile):
        return [
            (go(numbers_ref, numbers.at[tile], device), go(tile_ref, strip.at[:, tile], device))
            for device in (right, left, place.along_y(2))
        ]

    perm_tok = go(tok, held.at[0, place.p, core, xl], place.out_to())
    def to_scalars(source, tile, index):
        copy = pltpu.make_async_copy(source, numbers_sm.at[tile], meta_sems.at[index])
        copy.start()
        return copy

    def fill(which, tile, data):
        turned = jnp.concatenate([data[:, BLOCK:], data[:, :BLOCK]], axis=1)
        blocks[0:PAIRS] = data.reshape(PAIRS, BLOCK, 128)
        blocks[SHIFT : SHIFT + PAIRS] = turned.reshape(PAIRS, BLOCK, 128)
        for i in range(NB):
            for j in range(NB):
                half = (j % 2) * BLOCK
                dense[which, tile, i * BLOCK : (i + 1) * BLOCK, j * BLOCK : (j + 1) * BLOCK] = blocks[
                    numbers_sm[tile, which, i * NB + j], :, half : half + BLOCK
                ]

    def fill_tiles(tiles):
        def step(index, carry):
            which, tile = index % 2, tiles(index // 2)
            fill(which, tile, strip[which, tile])
            return carry

        return step

    zeros = jnp.zeros((BLOCK, 128), BF16)
    blocks[PAIRS] = zeros
    blocks[SHIFT + PAIRS] = zeros
    pre[...] = jnp.zeros_like(pre)
    slope_part[...] = jnp.zeros_like(slope_part)
    to_scalars(meta, mine, 0).wait()

    def fill_mine(which, carry):
        fill(which, mine, pay[which])
        return carry

    lax.fori_loop(0, 2, fill_mine, 0)

    def toks(step):
        return held.at[0, place.feature(step), core]

    def outs(step):
        return held.at[1, place.feature(step), core, xl]

    def both_outs(step):
        return held.at[1, place.feature(step), core]

    def to_core(ref):
        return go(ref, ref, place.sibling())

    lo_outs, core_toks, core_outs = {}, {}, {}

    def tile_at(step, side):
        return ((y + step + 4) % 4) * 2 + (xh + side) % 2

    def multiply(step):
        f = place.feature(step)
        t = held[0, f].reshape(GROUP, FEAT)
        pre[...] += jnp.dot(t, dense[0, f], preferred_element_type=F32)
        g = held[1, f].reshape(GROUP, FEAT)
        slope_part[...] += lax.dot_general(g, dense[1, f], (((1,), (1,)), ((), ())), preferred_element_type=F32)

    def multiply_ready(steps):
        for step in steps:
            core_toks[step].wait_recv()
            core_outs[step].wait_recv()

    perm_tok.wait_recv()
    piece = held.at[0, place.f, core, xl]

    def tok_pass(step, part_of, device):
        ref = held.at[0, place.feature(step), core, (xl + part_of) % 2]
        return go(ref, ref, device)

    lo_tok = go(piece, piece, place.partner_lo())
    right_tok = [tok_pass(0, 0, place.along_z(1))]
    left_tok = [tok_pass(0, 0, place.along_z(-1))]
    swap_meta = go(meta, numbers.at[mine], place.partner_hi())
    swap = go(pay, strip.at[:, mine], place.partner_hi())

    lo_tok.wait_recv()
    right_tok.append(tok_pass(0, 1, place.along_z(1)))
    left_tok.append(tok_pass(0, 1, place.along_z(-1)))
    core_toks[0] = to_core(toks(0))
    perm_out = go(out, held.at[1, place.p, core, xl], place.out_to())
    y_own = along_y(meta, pay, mine)

    swap_meta.wait_recv()
    twin_scalars = to_scalars(numbers.at[twin], twin, 1)
    swap.wait_recv()
    y_twin = along_y(numbers.at[twin], strip.at[:, twin], twin)
    twin_scalars.wait()

    def tok_step(step):
        for part_of in range(2):
            right_tok[part_of].wait_recv()
            if step < 4:
                right_tok[part_of] = tok_pass(-step, part_of, place.along_z(1))
            if step < 4:
                left_tok[part_of].wait_recv()
            if step < 3:
                left_tok[part_of] = tok_pass(step, part_of, place.along_z(-1))
        core_toks[4 if step == 4 else -step] = to_core(toks(-step))
        if step < 4:
            core_toks[step] = to_core(toks(step))

    def out_step(step):
        nonlocal right_out, left_out
        if step < 4:
            right_out.wait_recv()
            ref = outs(-step)
            if step < 3:
                right_out = go(ref, ref, place.along_z(1))
            lo_outs[-step] = go(ref, ref, place.partner_lo())
        left_out.wait_recv()
        ref = outs(step)
        if step < 4:
            left_out = go(ref, ref, place.along_z(-1))
        lo_outs[step] = go(ref, ref, place.partner_lo())

    def outs_to_core(steps):
        for step in steps:
            lo_outs[step].wait_recv()
            core_outs[step] = to_core(both_outs(step))

    def out_begin():
        perm_out.wait_recv()
        lo_outs[0] = go(outs(0), outs(0), place.partner_lo())
        return go(outs(0), outs(0), place.along_z(1)), go(outs(0), outs(0), place.along_z(-1))

    def tiles_came(came, side, first):
        scalars = []
        for number, step in enumerate((-1, 1, 2)):
            came[number][0].wait_recv()
            scalars.append(to_scalars(numbers.at[tile_at(step, side)], tile_at(step, side), first + number))
        for number in range(3):
            came[number][1].wait_recv()
            scalars[number].wait()

    def fill_along_y(side):
        lax.fori_loop(0, 6, fill_tiles(lambda index: tile_at(index + 1, side)), 0)

    tok_step(1)
    lax.fori_loop(0, 2, fill_tiles(lambda index: twin), 0)
    right_out, left_out = out_begin()
    tok_step(2)
    out_step(1)
    outs_to_core((0,))
    tok_step(3)
    out_step(2)
    outs_to_core((-1, 1))
    tok_step(4)
    out_step(3)
    outs_to_core((-2, 2))
    tiles_came(y_own, 0, 2)
    fill_along_y(0)
    out_step(4)
    outs_to_core((-3, 3))
    tiles_came(y_twin, 1, 5)
    fill_along_y(1)
    multiply_ready((0, -1, 1))

    def near_features(index, carry):
        multiply(index - 1)
        return carry

    lax.fori_loop(0, 3, near_features, 0)
    outs_to_core((4,))
    multiply_ready((-2, 2, -3, 3))

    def late_features(index, carry):
        multiply(2 + index + index // 2)
        return carry

    lax.fori_loop(0, 4, late_features, 0)
    multiply_ready((4,))
    multiply(4)

    def activate(index, carry):
        rows = pl.ds(pl.multiple_of(index * 32, 32), 32)
        v = pre[rows, :]
        t = jnp.tanh(GELU_C * (v + GELU_A * v * v * v))
        hidden[rows, :] = (0.5 * v * (1.0 + t)).astype(BF16)
        slope = 0.5 * (1.0 + t) + 0.5 * v * (1.0 - t * t) * GELU_C * (1.0 + 3.0 * GELU_A * v * v)
        pre_grad[rows, :] = (slope_part[rows, :] * slope).astype(BF16)
        return carry

    lax.fori_loop(0, GROUP // 32, activate, 0)

    def extract(product, which, tile):
        product = product.astype(BF16)
        for slab in range(5):
            data = product[:, slab * 128 : (slab + 1) * 128]
            turned = jnp.concatenate([data[:, BLOCK:], data[:, :BLOCK]], axis=1)
            grads[slab * NB : (slab + 1) * NB] = data.reshape(NB, BLOCK, 128)
            grads[SLAB + slab * NB : SLAB + (slab + 1) * NB] = turned.reshape(NB, BLOCK, 128)
        for slot in range(CAP):
            half = (slot % 2) * BLOCK
            at = (slot // 2) * BLOCK
            part[which, tile, at : at + BLOCK, half : half + BLOCK] = grads[
                numbers_sm[tile, 2 + which, slot], :, half : half + BLOCK
            ]

    def up_tile(tile):
        left_side = held[0, tile].reshape(GROUP, FEAT)
        extract(
            lax.dot_general(left_side, pre_grad[...], (((0,), (0,)), ((), ())), preferred_element_type=F32), 0, tile
        )

    def down_tile(tile):
        right_side = held[1, tile].reshape(GROUP, FEAT)
        extract(
            lax.dot_general(hidden[...], right_side, (((0,), (0,)), ((), ())), preferred_element_type=F32), 1, tile
        )

    half_rows = GROUP // 2

    def tok_feature(f, index):
        def rows_of(which_core):
            rows = pre_grad[pl.ds(pl.multiple_of(which_core * half_rows, half_rows), half_rows), :]
            return lax.dot_general(rows, dense[0, f], (((1,), (1,)), ((), ())), preferred_element_type=F32)

        core_send[f] = rows_of(1 - core).astype(BF16).reshape(2, TOK, FEAT)
        copies.copy(core_send.at[f], from_core.at[f], place.sibling(), index).start()
        own_tok[f] = rows_of(core).reshape(2, TOK, FEAT)

    core_first = copies.reserve(8)
    core_in = {}

    def tok_features(first, steps, step_of):
        def one(index, carry):
            tok_feature(place.feature(step_of(index)), core_first + first + index)
            return carry

        lax.fori_loop(0, len(steps), one, 0)
        for number, step in enumerate(steps):
            f = place.feature(step)
            core_in[step] = copies.started(
                core_send.at[f], from_core.at[f], place.sibling(), core_first + first + number
            )

    x_steps = (2, 1, -1, 0)
    x_first = copies.reserve(4)
    far_first = copies.reserve(2)
    near_first = copies.reserve(2)

    def x_send(slot, tile):
        up_tile(tile)
        copies.copy(part.at[0, tile], x_in.at[slot], place.partner_hi(), x_first + slot).start()

    def early_tiles(index, carry):
        x_send(index, tile_at(2 - index, 1))
        tile = tile_at(2, 1 - index)
        down_tile(tile)
        copies.copy(part.at[1, tile], y_far.at[1, 1 - index], left, far_first + index).start()
        return carry

    def next_tiles(index, carry):
        x_send(2 + index, tile_at(index - 1, 1))
        tile = tile_at(1, 1 - index)
        down_tile(tile)
        copies.copy(part.at[1, tile], y_right.at[1, 1 - index], right, near_first + index).start()
        return carry

    tok_features(0, (4, 3, -3), lambda index: 4 - index + (index // 2) * 3)
    lax.fori_loop(0, 2, early_tiles, 0)
    far_down = [
        copies.started(part.at[1, tile_at(2, side)], y_far.at[1, side], left, far_first + 1 - side) for side in range(2)
    ]

    f = place.feature(4)
    core_in[4].wait_recv()
    tok_send[0] = add(own_tok[f], from_core[f]).astype(BF16)
    go_right = go(tok_send.at[0, 0], right_far, place.along_z(1))
    go_left = go(tok_send.at[0, 1], left_far, place.along_z(-1))

    lax.fori_loop(0, 2, next_tiles, 0)
    down_right = [
        copies.started(part.at[1, tile_at(1, side)], y_right.at[1, side], right, near_first + 1 - side) for side in range(2)
    ]
    from_twin = {
        step: copies.started(part.at[0, tile_at(step, 1)], x_in.at[slot], place.partner_hi(), x_first + slot)
        for slot, step in enumerate(x_steps)
    }

    def pass_on(step):
        nonlocal go_right, go_left
        f = place.feature(step)
        core_in[step].wait_recv()
        go_right.wait_recv()
        slot = 2 * (4 - step) - 1
        if step == 3:
            tok_send[slot, 0] = add(own_tok[f, 0], from_core[f, 0], right_far[...]).astype(BF16)
            tok_send[slot, 1] = add(own_tok[f, 1], from_core[f, 1]).astype(BF16)
        else:
            tok_send[slot] = add(own_tok[f], from_core[f], right_in[2 - step]).astype(BF16)
        go_right = go(tok_send.at[slot], right_in.at[3 - step], place.along_z(1))
        f = place.feature(-step)
        core_in[-step].wait_recv()
        go_left.wait_recv()
        if step == 3:
            tok_send[slot + 1, 0] = add(own_tok[f, 0], from_core[f, 0]).astype(BF16)
            tok_send[slot + 1, 1] = add(own_tok[f, 1], from_core[f, 1], left_far[...]).astype(BF16)
        else:
            tok_send[slot + 1] = add(own_tok[f], from_core[f], left_in[2 - step]).astype(BF16)
        go_left = go(tok_send.at[slot + 1], left_in.at[3 - step], place.along_z(-1))

    pass_on(3)
    tok_features(3, (2, -2), lambda index: 2 + 4 * index)

    def more_tiles(index, carry):
        up_tile(tile_at(2 + index, 0))
        down_tile(tile_at(-1, 1 - index))
        return carry

    lax.fori_loop(0, 2, more_tiles, 0)
    from_twin[2].wait_recv()
    y_send[0, 0] = add(part[0, tile_at(2, 0)], x_in[0]).astype(BF16)
    far_up = go(y_send.at[0, 0], y_far.at[0, 0], right)
    down_left = [None, None]
    for side in (1, 0):
        far_down[side].wait_recv()
        y_send[1, side] = add(part[1, tile_at(-1, side)], y_far[1, side]).astype(BF16)
        down_left[side] = go(y_send.at[1, side], y_left.at[1, side], left)
    pass_on(2)
    from_twin[-1].wait_recv()
    y_send[0, 1] = add(part[0, tile_at(-1, 0)], x_in[2]).astype(BF16)
    up_left = go(y_send.at[0, 1], y_left.at[0, 0], left)

    tok_features(5, (1, -1, 0), lambda index: 1 + 6 * index - (index // 2) * 5)

    def last_tiles(index, carry):
        up_tile(tile_at(1 - index, 0))
        down_tile(tile_at(0, 1 - index))
        return carry

    lax.fori_loop(0, 2, last_tiles, 0)
    from_twin[1].wait_recv()
    far_up.wait_recv()
    y_send[0, 2] = add(part[0, tile_at(1, 0)], x_in[1], y_far[0, 0]).astype(BF16)
    up_right = go(y_send.at[0, 2], y_right.at[0, 0], right)
    pass_on(1)

    down_left[1].wait_recv()
    down_right[1].wait_recv()
    hi_out[...] = add(part[1, twin], y_left[1, 1], y_right[1, 1]).astype(BF16)
    hi = go(hi_out, hi_in, place.partner_hi())

    def put(target, total, counts):
        pairs[...] = total.reshape(PAIRS, BLOCK, 128)
        slot = 2 * lax.broadcasted_iota(jnp.int32, (PAIRS, 128), 0)
        even_live, odd_live = slot < counts[0, 0], slot + 1 < counts[0, 0]
        for k in range(BLOCK // 2):
            low, high = pairs[:, 2 * k, :], pairs[:, 2 * k + 1, :]
            even = jnp.concatenate([low[:, :BLOCK], high[:, :BLOCK]], axis=1)
            odd = jnp.concatenate([low[:, BLOCK:], high[:, BLOCK:]], axis=1)
            wide[k, pl.ds(0, PAIRS, stride=2), :] = jnp.where(even_live, even, 0.0)
            wide[k, pl.ds(1, PAIRS, stride=2), :] = jnp.where(odd_live, odd, 0.0)
            target[0, 0, :, k * 128 : (k + 1) * 128] = wide[k, 0:CAP, :]

    from_twin[0].wait_recv()
    up_left.wait_recv()
    up_right.wait_recv()
    put(up_out, add(part[0, mine], x_in[3], y_left[0, 0], y_right[0, 0]), up_counts)

    f = place.f
    core_in[0].wait_recv()
    go_right.wait_recv()
    go_left.wait_recv()
    other = 1 - xl
    lo_out[...] = add(own_tok[f, other], from_core[f, other], right_in[2, other], left_in[2, other]).astype(BF16)
    lo = go(lo_out, lo_in, place.partner_lo())

    down_left[0].wait_recv()
    down_right[0].wait_recv()
    lo.wait_recv()
    home[...] = add(own_tok[f, xl], from_core[f, xl], right_in[2, xl], left_in[2, xl], lo_in[...]).astype(BF16)
    back = go(home, tok_out, place.back_to())

    hi.wait_recv()
    put(down_out, add(part[1, mine], y_left[1, 0], y_right[1, 0], hi_in[...]), down_counts)
    back.wait_recv()
    copies.finish()
    assert copies.number == COPIES, copies.number


COPIES = 94


def vmem(count):
    return [pl.BlockSpec(memory_space=pltpu.VMEM)] * count


def sds(shape, dtype=BF16):
    return jax.ShapeDtypeStruct(shape, dtype)


def offsets(up_layout, up_counts, down_layout, down_counts):
    up_ids, down_ids = up_layout[0, 0], down_layout[0, 0]
    ids = jnp.stack([up_ids, (down_ids % NB) * NB + down_ids // NB])
    counts = jnp.stack([up_counts[0, 0], down_counts[0, 0]])
    numbers = jnp.arange(128, dtype=jnp.int32)
    slots = numbers[:CAP]
    hit = (ids[:, :, None] == numbers) & (slots[None, :] < counts[:, None])[:, :, None]
    slot_of = CAP + jnp.sum(jnp.where(hit, slots[None, :, None] - CAP, 0), axis=1)
    place = ((slot_of + numbers % NB) % 2) * SHIFT + slot_of // 2
    row, lane = ids // NB, ids % NB
    take = ((lane + slots) % 2) * SLAB + (lane // 2) * NB + row
    take = jnp.pad(take, ((0, 0), (0, 128 - CAP)))
    return jnp.concatenate([place, take, jnp.zeros((4, 128), jnp.int32)], axis=0)


def body(tokens, up_blocks, up_layout, up_counts, down_blocks, down_layout, down_counts, grad_out):
    meta = offsets(up_layout, up_counts, down_layout, down_counts)
    tile = (ROWS, 128)
    scalar = [pl.BlockSpec(memory_space=pltpu.SMEM)]
    piece = (TOK, FEAT)
    return pl.pallas_call(
        kernel,
        out_shape=(sds(piece), sds((1, 1, CAP, BLOCK * BLOCK), F32), sds((1, 1, CAP, BLOCK * BLOCK), F32)),
        in_specs=vmem(4) + scalar + vmem(1) + scalar,
        out_specs=tuple(vmem(3)),
        scratch_shapes=[
            pltpu.VMEM((2,) + tile, BF16),
            pltpu.VMEM((BLOCK // 2, CAP + 2, 128), F32),
            pltpu.VMEM((PAIRS, BLOCK, 128), F32),
            pltpu.VMEM((2, 8, 2, 2) + piece, BF16),
            pltpu.VMEM((2, 8) + tile, BF16),
            pltpu.VMEM((8, 8, 128), jnp.int32),
            pltpu.SMEM((8, 8, 128), jnp.int32),
            pltpu.VMEM((2, 8, FEAT, FEAT), BF16),
            pltpu.VMEM((2 * SHIFT, BLOCK, 128), BF16),
            pltpu.VMEM((GROUP, FEAT), F32),
            pltpu.VMEM((GROUP, FEAT), F32),
            pltpu.VMEM((GROUP, FEAT), BF16),
            pltpu.VMEM((GROUP, FEAT), BF16),
            pltpu.VMEM((2 * SLAB, BLOCK, 128), BF16),
            pltpu.VMEM((8, 2) + piece, F32),
            pltpu.VMEM((8, 2) + piece, BF16),
            pltpu.VMEM((8, 2) + piece, BF16),
            pltpu.VMEM((7, 2) + piece, BF16),
            pltpu.VMEM((3, 2) + piece, BF16),
            pltpu.VMEM((3, 2) + piece, BF16),
            pltpu.VMEM(piece, BF16),
            pltpu.VMEM(piece, BF16),
            pltpu.VMEM(piece, BF16),
            pltpu.VMEM(piece, BF16),
            pltpu.VMEM(piece, BF16),
            pltpu.VMEM((2, 8) + tile, BF16),
            pltpu.VMEM((4,) + tile, BF16),
            pltpu.VMEM((2, 2) + tile, BF16),
            pltpu.VMEM((2, 2) + tile, BF16),
            pltpu.VMEM((2, 2) + tile, BF16),
            pltpu.VMEM((2, 3) + tile, BF16),
            pltpu.VMEM(tile, BF16),
            pltpu.VMEM(tile, BF16),
            pltpu.SemaphoreType.DMA((8,)),
            pltpu.SemaphoreType.DMA((COPIES,)),
            pltpu.SemaphoreType.DMA((COPIES,)),
        ],
        compiler_params=pltpu.CompilerParams(collective_id=0, has_side_effects=True, vmem_limit_bytes=60 * 2**20),
        name="layer",
    )(tokens, grad_out, meta, up_blocks, up_counts, down_blocks, down_counts)


def solution(mesh):
    in_specs = (
        P("col", "row"),
        P("row", "col", None, None),
        P("row", "col", None),
        P("row", "col"),
        P("row", "col", None, None),
        P("row", "col", None),
        P("row", "col"),
        P("col", "row"),
    )
    out_specs = (P("col", "row"), P("row", "col", None, None), P("row", "col", None, None))
    return jax.shard_map(body, mesh=mesh, in_specs=in_specs, out_specs=out_specs, check_vma=False)
```
